32 devices in a mesh: dp: 8 (over z, core), tensor: 4 (over y, x).
Axes of the slice: x: 2, y: 2, z: 4, core: 2. Of those that a mesh axis runs over, the one named last changes fastest.
Arguments:
- policy: bfloat16 [8, 1024, 16384], P('dp', 'tensor'), may hold values from -4 to 4
- ref_weight: bfloat16 [8192, 16384], P('tensor', 'dp'), may hold values from -4 to 4
- tokens: bfloat16 [2, 384, 8192], P(None, 'dp', 'tensor'), may hold values from -400 to 400
- gain: float32 [8192], P('tensor'), may hold values from 0.5 to 2
Outputs:
- blended: bfloat16 [8192, 16384], P('tensor', 'dp')
- activated: bfloat16 [2, 384, 16384], P(None, 'tensor', 'dp')
The draws below stay inside these ranges and needn't reach their ends.
All inputs are finite; a program needn't handle non-finite values.
Results may differ from the reference program's by a relative error of at most 0.022.
Values may be sent and summed in bfloat16 or wider, within the bound.
A program may use at most 128 MiB of HBM per device.

```python
import math
import jax
import jax.numpy as jnp
from jax import lax

D = 8192
FF = 16384
MICRO = 2
TOKENS = 384
N_DP = 8
N_TENSOR = 4


def draw_tokens(key, part):
    key = jax.random.fold_in(key, 11)
    key_val, key_row, key_col = jax.random.split(key, 3)
    values = jnp.clip(jax.random.normal(key_val, (MICRO, TOKENS, D), jnp.float32), -4.0, 4.0)
    row_scale = 10.0 ** jax.random.uniform(key_row, (MICRO, TOKENS, 1), jnp.float32)
    ramp = jnp.arange(D, dtype=jnp.float32) / D
    col_scale = 10.0 ** (0.5 * ramp + 0.5 * jax.random.uniform(key_col, (D,), jnp.float32))
    return (values * row_scale * col_scale).astype(jnp.bfloat16)


def shard_levels(stream_key, shape, cuts, low, largest):
    factor_of = 1.0
    for position, shards_of in cuts:
        heights = jax.random.uniform(jax.random.fold_in(jax.random.fold_in(stream_key, 6), position), (shards_of,), jnp.float32, low / len(cuts), largest / len(cuts))
        factor_of = factor_of * jnp.repeat(jnp.exp(heights), shape[position] // shards_of).reshape((-1,) + (1,) * (len(shape) - 1 - position))
    return factor_of


def gaussian(rng, extent, scale, most, shards=(), kind=jnp.bfloat16):
    values = scale * jax.random.normal(rng, extent, jnp.float32)
    if shards:
        values = values * shard_levels(rng, extent, shards, -0.22, 0.18)
    return jnp.clip(values, -most, most).astype(kind)


def setup_inputs(seed: int = 0) -> dict:
    key_of = jax.random.split(jax.random.key(seed), 5)
    policy = gaussian(key_of[0], (N_DP, D // N_DP, FF), 1.0, 4.0, ((0, 8), (1, 4)))
    ref_weight = gaussian(key_of[1], (D, FF), 1.0, 4.0, ((0, 4), (1, 8)))
    tokens = draw_tokens(jax.random.fold_in(key_of[4], 71), 0)
    gain = jnp.clip(jnp.exp(math.log(2.0) - 1.3862944 * jax.random.uniform(key_of[3], (D,), jnp.float32) ** shard_levels(key_of[3], (D,), ((0, 4),), -0.2, 0.2)), 0.5, 2.0)
    return dict(policy=policy, ref_weight=ref_weight, tokens=tokens, gain=gain)


ema_rate = 0.5
norm_eps = 1e-06

def reference(policy, ref_weight, tokens, gain):
    shard_rows = D // (N_DP * N_TENSOR)
    policy_matrix = policy.reshape(N_DP, N_TENSOR, shard_rows, FF).transpose(1, 0, 2, 3).reshape(D, FF)
    ref_f = ref_weight.astype(jnp.float32)
    blended = (ref_f + ema_rate * (policy_matrix.astype(jnp.float32) - ref_f)).astype(jnp.bfloat16)
    tok_f = tokens.astype(jnp.float32)
    squares = lax.optimization_barrier(jnp.sum(tok_f * tok_f, axis=2, keepdims=True))
    normed = (tok_f * lax.rsqrt(squares / D + norm_eps) * gain).astype(jnp.bfloat16)
    normed = normed.reshape(MICRO * TOKENS, D)
    local_width = D // N_TENSOR
    out_scale = 1.0 / math.sqrt(D)

    def add_block(index, summed):
        offset = (index * local_width).astype(jnp.int32)
        columns = lax.dynamic_slice_in_dim(normed, offset, local_width, 1)
        weights = lax.dynamic_slice_in_dim(blended, offset, local_width, 0)
        partial_term = jnp.dot(columns, weights, preferred_element_type=jnp.float32) * out_scale
        rounded = lax.optimization_barrier(partial_term.astype(jnp.bfloat16))
        return summed + rounded.astype(jnp.float32)
    summed = lax.fori_loop(0, N_TENSOR, add_block, jnp.zeros((MICRO * TOKENS, FF), jnp.float32))
    activated = jax.nn.silu(summed).astype(jnp.bfloat16).reshape(MICRO, TOKENS, FF)
    return (blended, activated)
```

```python
import functools
import math

import jax
import jax.numpy as jnp
from jax import lax
from jax.experimental import pallas as pl
from jax.experimental.pallas import tpu as pltpu
from jax.sharding import PartitionSpec as P

MESH = pl.DeviceIdType.MESH
LANES = 128
AHEAD = 2

ema_rate = 0.5
norm_eps = 1e-06


def each(count, step):
    lax.fori_loop(0, count, lambda i, _: (step(i), 0)[1], 0)


def fused_kernel(
    plan,
    policy,
    ref_in,
    tokens,
    gain,
    blended,
    activated,
    arrived,
    weights,
    tok,
    squares,
    gathered,
    partial,
    terms,
    piece_send,
    piece_recv,
    own_sem,
    ref_sem,
    out_sem,
    tok_sem,
    square_send,
    square_recv,
    up_send,
    down_send,
    pair_send,
    block_recv,
    term_send,
    term_recv,
):
    dp, tensor, chunks, width, model = plan
    me = lax.axis_index("dp")
    col = lax.axis_index("tensor")
    levels = dp // 2
    level = me // 2
    core = me % 2
    pair = me + 1 - 2 * core
    per_owner = dp // tensor
    micros, per_micro, features = tokens.shape
    rows = micros * per_micro
    columns = chunks * width

    barrier = pltpu.get_barrier_semaphore()
    for off in range(1, dp):
        pl.semaphore_signal(
            barrier, inc=1, device_id={"dp": (me + off) % dp}, device_id_type=MESH
        )
    for off in range(1, tensor):
        pl.semaphore_signal(
            barrier, inc=1, device_id={"tensor": (col + off) % tensor}, device_id_type=MESH
        )

    def own_piece(c):
        return pltpu.make_async_copy(
            policy.at[:, pl.ds(pl.multiple_of(me * columns + c * width, width), width)],
            arrived.at[c, me],
            own_sem.at[c],
        )

    def ref_piece(c):
        return pltpu.make_async_copy(
            ref_in.at[:, :, pl.ds(pl.multiple_of(c * width, width), width)],
            weights.at[c],
            ref_sem.at[c],
        )

    def out_piece(c):
        return pltpu.make_async_copy(
            weights.at[c],
            blended.at[:, :, pl.ds(pl.multiple_of(c * width, width), width)],
            out_sem.at[c],
        )

    def send_piece(c, other):
        return pltpu.make_async_remote_copy(
            src_ref=policy.at[
                :, pl.ds(pl.multiple_of(other * columns + c * width, width), width)
            ],
            dst_ref=arrived.at[c, me],
            send_sem=piece_send.at[c, other],
            recv_sem=piece_recv.at[c, me],
            device_id={"dp": other},
            device_id_type=MESH,
        )

    def take_piece(c, other):
        return pltpu.make_async_remote_copy(
            src_ref=policy.at[:, pl.ds(0, width)],
            dst_ref=arrived.at[c, other],
            send_sem=piece_send.at[c, other],
            recv_sem=piece_recv.at[c, other],
            device_id={"dp": other},
            device_id_type=MESH,
        )

    def send_squares(other):
        return pltpu.make_async_remote_copy(
            src_ref=squares.at[col],
            dst_ref=squares.at[col],
            send_sem=square_send.at[other],
            recv_sem=square_recv.at[col],
            device_id={"tensor": other},
            device_id_type=MESH,
        )

    def take_squares(other):
        return pltpu.make_async_remote_copy(
            src_ref=squares.at[other],
            dst_ref=squares.at[other],
            send_sem=square_send.at[other],
            recv_sem=square_recv.at[other],
            device_id={"tensor": other},
            device_id_type=MESH,
        )

    def block_copy(block, sem, other):
        return pltpu.make_async_remote_copy(
            src_ref=gathered.at[block],
            dst_ref=gathered.at[block],
            send_sem=sem,
            recv_sem=block_recv.at[block],
            device_id={"dp": other},
            device_id_type=MESH,
        )

    def send_term(c, other):
        return pltpu.make_async_remote_copy(
            src_ref=partial.at[c, pl.ds(other * per_owner, per_owner)],
            dst_ref=terms.at[c, col],
            send_sem=term_send.at[c, other],
            recv_sem=term_recv.at[c, col],
            device_id={"tensor": other},
            device_id_type=MESH,
        )

    def take_term(c, other):
        return pltpu.make_async_remote_copy(
            src_ref=partial.at[c, pl.ds(other * per_owner, per_owner)],
            dst_ref=terms.at[c, other],
            send_sem=term_send.at[c, other],
            recv_sem=term_recv.at[c, other],
            device_id={"tensor": other},
            device_id_type=MESH,
        )

    tok_copy = pltpu.make_async_copy(tokens, tok, tok_sem)
    tok_copy.start()
    each(chunks, lambda c: ref_piece(c).start())
    each(chunks, lambda c: own_piece(c).start())
    tok_copy.wait()
    for m in range(micros):
        total = jnp.zeros((per_micro, LANES), jnp.float32)
        for f in range(features // LANES):
            part = tok[m, :, f * LANES : (f + 1) * LANES].astype(jnp.float32)
            total = total + part * part
        squares[col, m * per_micro : (m + 1) * per_micro, :] = total
    pl.semaphore_wait(barrier, dp + tensor - 2)

    for off in range(1, tensor):
        send_squares((col + off) % tensor).start()

    order = sorted(range(1, dp), key=lambda off: abs(off - dp // 2))

    def send_chunk(c):
        for off in order:
            send_piece(c, (me + off) % dp).start()

    for c in range(AHEAD):
        send_chunk(c)

    for off in range(1, tensor):
        take_squares((col + off) % tensor).wait_recv()
    for m in range(micros):
        total = squares[0, m * per_micro : (m + 1) * per_micro, :]
        for t in range(1, tensor):
            total = total + squares[t, m * per_micro : (m + 1) * per_micro, :]
        scale = lax.rsqrt(jnp.sum(total, axis=1, keepdims=True) / model + norm_eps)
        for f in range(0, features, 512):
            span = min(512, features - f)
            gathered[me, m * per_micro : (m + 1) * per_micro, f : f + span] = (
                tok[m, :, f : f + span].astype(jnp.float32) * scale * gain[:, f : f + span]
            ).astype(jnp.bfloat16)

    def relay(step, act):
        below = level - step
        above = level + step

        @pl.when(below >= 0)
        def _():
            block = 2 * below + core
            if step > 0:
                act("take", block_copy(block, up_send.at[step], me))

            @pl.when(level + 1 < levels)
            def _():
                act("send", block_copy(block, up_send.at[step], (me + 2) % dp))

            act("send", block_copy(block, pair_send.at[below], pair))

        @pl.when(above < levels)
        def _():
            block = 2 * above + core
            if step > 0:
                act("take", block_copy(block, down_send.at[step], me))
                act("send", block_copy(block, pair_send.at[above], pair))

            @pl.when(level > 0)
            def _():
                act("send", block_copy(block, down_send.at[step], (me + dp - 2) % dp))

    def forward(kind, copy):
        copy.wait_recv() if kind == "take" else copy.start()

    def settle(kind, copy):
        if kind == "send":
            copy.wait_send()

    relay(0, forward)

    def take_chunk(c):
        ref_piece(c).wait()
        own_piece(c).wait()
        for off in range(1, dp):
            take_piece(c, (me + off) % dp).wait_recv()

        def blend(d):
            old = weights[c, d].astype(jnp.float32)
            new = arrived[c, d].astype(jnp.float32)
            weights[c, d] = (old + ema_rate * (new - old)).astype(jnp.bfloat16)

        each(dp, blend)
        out_piece(c).start()

    out_scale = 1.0 / math.sqrt(model)

    def multiply(c):
        left = gathered[...].reshape(dp * rows, features)
        right = weights[c].reshape(features, width)
        product = jnp.dot(left, right, preferred_element_type=jnp.float32) * out_scale
        partial[c] = product.astype(jnp.bfloat16).reshape(dp, rows, width)
        for off in range(1, tensor):
            send_term(c, (col + off) % tensor).start()

    def finish(c):
        for off in range(1, tensor):
            take_term(c, (col + off) % tensor).wait_recv()
        for b in range(per_owner):
            gate = partial[c, col * per_owner + b].astype(jnp.float32)
            for off in range(1, tensor):
                gate = gate + terms[c, (col + off) % tensor, b].astype(jnp.float32)
            result = (gate / (1.0 + jnp.exp(-gate))).astype(jnp.bfloat16)
            for m in range(micros):
                activated[
                    m,
                    pl.ds(b * per_micro, per_micro),
                    pl.ds(pl.multiple_of(c * width, width), width),
                ] = result[m * per_micro : (m + 1) * per_micro]

    early = levels
    for c in range(early):
        if c + AHEAD < chunks:
            send_chunk(c + AHEAD)
        take_chunk(c)
        if c + 1 < levels:
            relay(c + 1, forward)
    each(levels, lambda z: block_copy(2 * z + 1 - core, pair_send.at[z], pair).wait_recv())
    each(early, multiply)

    def late(c):
        c = c + early

        @pl.when(c + AHEAD < chunks)
        def _():
            send_chunk(c + AHEAD)

        take_chunk(c)
        multiply(c)
        finish(c - early)

    each(chunks - early, late)
    each(early, lambda c: finish(c + chunks - early))

    for off in range(1, tensor):
        send_squares((col + off) % tensor).wait_send()
    for step in range(levels):
        relay(step, settle)

    def settle_chunk(c):
        out_piece(c).wait()
        for off in range(1, dp):
            send_piece(c, (me + off) % dp).wait_send()
        for off in range(1, tensor):
            send_term(c, (col + off) % tensor).wait_send()

    each(chunks, settle_chunk)


def fused(policy, ref_weight, tokens, gain, dp, tensor, chunks, model):
    _, piece_rows, _ = policy.shape
    local, columns = ref_weight.shape
    micros, per_micro, features = tokens.shape
    rows = micros * per_micro
    per_owner = dp // tensor
    width = columns // chunks
    bf16, f32 = jnp.bfloat16, jnp.float32
    plan = (dp, tensor, chunks, width, model)
    dma = pltpu.SemaphoreType.DMA
    blended, activated = pl.pallas_call(
        functools.partial(fused_kernel, plan),
        out_shape=[
            jax.ShapeDtypeStruct((dp, piece_rows, columns), bf16),
            jax.ShapeDtypeStruct((micros, per_owner * per_micro, columns), bf16),
        ],
        in_specs=[
            pl.BlockSpec(memory_space=pl.ANY),
            pl.BlockSpec(memory_space=pl.ANY),
            pl.BlockSpec(memory_space=pl.ANY),
            pl.BlockSpec(memory_space=pltpu.VMEM),
        ],
        out_specs=[
            pl.BlockSpec(memory_space=pl.ANY),
            pl.BlockSpec(memory_space=pltpu.VMEM),
        ],
        scratch_shapes=[
            pltpu.VMEM((chunks, dp, piece_rows, width), bf16),
            pltpu.VMEM((chunks, dp, piece_rows, width), bf16),
            pltpu.VMEM((micros, per_micro, features), bf16),
            pltpu.VMEM((tensor, rows, LANES), f32),
            pltpu.VMEM((dp, rows, features), bf16),
            pltpu.VMEM((chunks, dp, rows, width), bf16),
            pltpu.VMEM((chunks, tensor, per_owner, rows, width), bf16),
            dma((chunks, dp)),
            dma((chunks, dp)),
            dma((chunks,)),
            dma((chunks,)),
            dma((chunks,)),
            dma,
            dma((tensor,)),
            dma((tensor,)),
            dma((dp // 2,)),
            dma((dp // 2,)),
            dma((dp // 2,)),
            dma((dp,)),
            dma((chunks, tensor)),
            dma((chunks, tensor)),
        ],
        compiler_params=pltpu.CompilerParams(
            collective_id=0, has_side_effects=True, vmem_limit_bytes=52 * 1024 * 1024
        ),
        cost_estimate=pl.CostEstimate(
            flops=2 * dp * rows * features * columns,
            bytes_accessed=10 * local * columns,
            transcendentals=per_owner * rows * columns,
        ),
    )(
        policy.reshape(piece_rows, dp * columns),
        ref_weight.reshape(dp, piece_rows, columns),
        tokens,
        gain.reshape(1, features),
    )
    return blended.reshape(local, columns), activated


def plain(policy, ref_weight, tokens, gain, tensor, model):
    arrived = lax.all_to_all(policy, "dp", split_axis=2, concat_axis=0, tiled=True)
    new = arrived.reshape(ref_weight.shape).astype(jnp.float32)
    old = ref_weight.astype(jnp.float32)
    blended = (old + ema_rate * (new - old)).astype(jnp.bfloat16)
    pieces = []
    for micro in range(tokens.shape[0]):
        values = tokens[micro].astype(jnp.float32)
        total = lax.psum(jnp.sum(values * values, axis=1, keepdims=True), "tensor")
        normed = (values * lax.rsqrt(total / model + norm_eps) * gain).astype(jnp.bfloat16)
        normed = lax.all_gather(normed, "dp", axis=0, tiled=True)
        term = jnp.dot(normed, blended, preferred_element_type=jnp.float32)
        term = (term * (1.0 / math.sqrt(model))).astype(jnp.bfloat16)
        pieces.append(lax.psum_scatter(term, "tensor", scatter_dimension=0, tiled=True))
    gate = jnp.stack(pieces).astype(jnp.float32)
    return blended, jax.nn.silu(gate).astype(jnp.bfloat16)


def solution(mesh):
    dp, tensor = mesh.shape["dp"], mesh.shape["tensor"]

    def body(policy, ref_weight, tokens, gain):
        local, columns = ref_weight.shape
        model = local * tensor
        chunks = columns // 256
        fits = (
            dp % (2 * tensor) == 0
            and policy.shape[1] % 16 == 0
            and tokens.shape[1] % 16 == 0
            and columns % 256 == 0
            and chunks > dp // 2
            and dp // 2 >= AHEAD
        )
        if fits:
            return fused(policy, ref_weight, tokens, gain, dp, tensor, chunks, model)
        return plain(policy, ref_weight, tokens, gain, tensor, model)

    return jax.shard_map(
        body,
        mesh=mesh,
        in_specs=(P("dp", "tensor", None), P("tensor", "dp"), P(None, "dp", "tensor"), P("tensor")),
        out_specs=(P("tensor", "dp"), P(None, "tensor", "dp")),
        check_vma=False,
    )
```

```python
import functools
import math

import jax
import jax.numpy as jnp
from jax import lax
from jax.experimental import pallas as pl
from jax.experimental.pallas import tpu as pltpu
from jax.sharding import PartitionSpec as P

MESH = pl.DeviceIdType.MESH
LANES = 128
AHEAD = 2

ema_rate = 0.5
norm_eps = 1e-06


def each(count, step):
    lax.fori_loop(0, count, lambda i, _: (step(i), 0)[1], 0)


def fused_kernel(
    plan,
    policy,
    ref_in,
    tokens,
    gain,
    blended,
    activated,
    arrived,
    tok,
    gains,
    squares,
    gathered,
    partial,
    terms,
    piece_send,
    piece_recv,
    own_sem,
    ref_sem,
    tok_sem,
    gain_sem,
    square_send,
    square_recv,
    up_send,
    down_send,
    pair_send,
    block_recv,
    term_send,
    term_recv,
):
    dp, tensor, chunks, width, model = plan
    me = lax.axis_index("dp")
    col = lax.axis_index("tensor")
    levels = dp // 2
    level = me // 2
    core = me % 2
    pair = me + 1 - 2 * core
    per_owner = dp // tensor
    micros, per_micro, features = tokens.shape
    rows = micros * per_micro
    columns = chunks * width

    barrier = pltpu.get_barrier_semaphore()
    for off in range(1, dp):
        pl.semaphore_signal(
            barrier, inc=1, device_id={"dp": (me + off) % dp}, device_id_type=MESH
        )
    for off in range(1, tensor):
        pl.semaphore_signal(
            barrier, inc=1, device_id={"tensor": (col + off) % tensor}, device_id_type=MESH
        )

    def own_piece(c):
        return pltpu.make_async_copy(
            policy.at[:, pl.ds(pl.multiple_of(me * columns + c * width, width), width)],
            arrived.at[c, me],
            own_sem.at[c],
        )

    def part_of(c):
        return pl.ds(pl.multiple_of(c * width, width), width)

    def ref_piece(c):
        return pltpu.make_async_copy(
            ref_in.at[:, :, part_of(c)], blended.at[:, :, part_of(c)], ref_sem.at[c]
        )

    def send_piece(c, other):
        return pltpu.make_async_remote_copy(
            src_ref=policy.at[
                :, pl.ds(pl.multiple_of(other * columns + c * width, width), width)
            ],
            dst_ref=arrived.at[c, me],
            send_sem=piece_send.at[c, other],
            recv_sem=piece_recv.at[c, me],
            device_id={"dp": other},
            device_id_type=MESH,
        )

    def take_piece(c, other):
        return pltpu.make_async_remote_copy(
            src_ref=policy.at[:, pl.ds(0, width)],
            dst_ref=arrived.at[c, other],
            send_sem=piece_send.at[c, other],
            recv_sem=piece_recv.at[c, other],
            device_id={"dp": other},
            device_id_type=MESH,
        )

    def send_squares(other):
        return pltpu.make_async_remote_copy(
            src_ref=squares.at[col],
            dst_ref=squares.at[col],
            send_sem=square_send.at[other],
            recv_sem=square_recv.at[col],
            device_id={"tensor": other},
            device_id_type=MESH,
        )

    def take_squares(other):
        return pltpu.make_async_remote_copy(
            src_ref=squares.at[other],
            dst_ref=squares.at[other],
            send_sem=square_send.at[other],
            recv_sem=square_recv.at[other],
            device_id={"tensor": other},
            device_id_type=MESH,
        )

    def block_copy(block, sem, other):
        return pltpu.make_async_remote_copy(
            src_ref=gathered.at[block],
            dst_ref=gathered.at[block],
            send_sem=sem,
            recv_sem=block_recv.at[block],
            device_id={"dp": other},
            device_id_type=MESH,
        )

    def send_term(c, other):
        return pltpu.make_async_remote_copy(
            src_ref=partial.at[c, pl.ds(other * per_owner, per_owner)],
            dst_ref=terms.at[c, col],
            send_sem=term_send.at[c, other],
            recv_sem=term_recv.at[c, col],
            device_id={"tensor": other},
            device_id_type=MESH,
        )

    def take_term(c, other):
        return pltpu.make_async_remote_copy(
            src_ref=partial.at[c, pl.ds(other * per_owner, per_owner)],
            dst_ref=terms.at[c, other],
            send_sem=term_send.at[c, other],
            recv_sem=term_recv.at[c, other],
            device_id={"tensor": other},
            device_id_type=MESH,
        )

    tok_copy = pltpu.make_async_copy(tokens, tok, tok_sem)
    gain_copy = pltpu.make_async_copy(gain, gains, gain_sem)
    tok_copy.start()
    gain_copy.start()
    each(chunks, lambda c: ref_piece(c).start())
    each(chunks, lambda c: own_piece(c).start())
    tok_copy.wait()
    gain_copy.wait()
    for m in range(micros):
        total = jnp.zeros((per_micro, LANES), jnp.float32)
        for f in range(features // LANES):
            part = tok[m, :, f * LANES : (f + 1) * LANES].astype(jnp.float32)
            total = total + part * part
        squares[col, m * per_micro : (m + 1) * per_micro, :] = total
    pl.semaphore_wait(barrier, dp + tensor - 2)

    for off in range(1, tensor):
        send_squares((col + off) % tensor).start()

    order = sorted(range(1, dp), key=lambda off: abs(off - dp // 2))

    def send_chunk(c):
        for off in order:
            send_piece(c, (me + off) % dp).start()

    for c in range(AHEAD):
        send_chunk(c)

    for off in range(1, tensor):
        take_squares((col + off) % tensor).wait_recv()
    for m in range(micros):
        total = squares[0, m * per_micro : (m + 1) * per_micro, :]
        for t in range(1, tensor):
            total = total + squares[t, m * per_micro : (m + 1) * per_micro, :]
        scale = lax.rsqrt(jnp.sum(total, axis=1, keepdims=True) / model + norm_eps)
        for f in range(0, features, 512):
            span = min(512, features - f)
            gathered[me, m * per_micro : (m + 1) * per_micro, f : f + span] = (
                tok[m, :, f : f + span].astype(jnp.float32) * scale * gains[:, f : f + span]
            ).astype(jnp.bfloat16)

    def relay(step, act):
        below = level - step
        above = level + step

        @pl.when(below >= 0)
        def _():
            block = 2 * below + core
            if step > 0:
                act("take", block_copy(block, up_send.at[step], me))

            @pl.when(level + 1 < levels)
            def _():
                act("send", block_copy(block, up_send.at[step], (me + 2) % dp))

            act("send", block_copy(block, pair_send.at[below], pair))

        @pl.when(above < levels)
        def _():
            block = 2 * above + core
            if step > 0:
                act("take", block_copy(block, down_send.at[step], me))
                act("send", block_copy(block, pair_send.at[above], pair))

            @pl.when(level > 0)
            def _():
                act("send", block_copy(block, down_send.at[step], (me + dp - 2) % dp))

    def forward(kind, copy):
        copy.wait_recv() if kind == "take" else copy.start()

    def settle(kind, copy):
        if kind == "send":
            copy.wait_send()

    relay(0, forward)

    def take_chunk(c):
        ref_piece(c).wait()
        own_piece(c).wait()

        def blend(d):
            old = blended[d, :, part_of(c)].astype(jnp.float32)
            new = arrived[c, d].astype(jnp.float32)
            blended[d, :, part_of(c)] = (old + ema_rate * (new - old)).astype(jnp.bfloat16)

        blend(me)

        def take(i):
            other = (me + i + 1) % dp
            take_piece(c, other).wait_recv()
            blend(other)

        each(dp - 1, take)

    out_scale = 1.0 / math.sqrt(model)

    def multiply(c):
        left = gathered[...].reshape(dp * rows, features)
        right = blended[:, :, part_of(c)].reshape(features, width)
        product = jnp.dot(left, right, preferred_element_type=jnp.float32) * out_scale
        partial[c] = product.astype(jnp.bfloat16).reshape(dp, rows, width)
        for off in range(1, tensor):
            send_term(c, (col + off) % tensor).start()

    def finish(c):
        for off in range(1, tensor):
            take_term(c, (col + off) % tensor).wait_recv()
        for b in range(per_owner):
            gate = partial[c, col * per_owner + b].astype(jnp.float32)
            for off in range(1, tensor):
                gate = gate + terms[c, (col + off) % tensor, b].astype(jnp.float32)
            result = (gate / (1.0 + jnp.exp(-gate))).astype(jnp.bfloat16)
            for m in range(micros):
                activated[
                    m,
                    pl.ds(b * per_micro, per_micro),
                    part_of(c),
                ] = result[m * per_micro : (m + 1) * per_micro]

    early = levels
    for c in range(early):
        if c + AHEAD < chunks:
            send_chunk(c + AHEAD)
        take_chunk(c)
        if c + 1 < levels:
            relay(c + 1, forward)
    each(levels, lambda z: block_copy(2 * z + 1 - core, pair_send.at[z], pair).wait_recv())
    each(early, multiply)

    def late(c):
        c = c + early

        @pl.when(c + AHEAD < chunks)
        def _():
            send_chunk(c + AHEAD)

        take_chunk(c)
        multiply(c)
        first = 2 * (c - early)
        each(2, lambda i: pl.when(first + i < c)(lambda: finish(first + i)))

    each(chunks - early, late)
    done = min(2 * (chunks - early), chunks - 1)
    each(chunks - done, lambda i: finish(done + i))

    for off in range(1, tensor):
        send_squares((col + off) % tensor).wait_send()
    for step in range(levels):
        relay(step, settle)

    def settle_chunk(c):
        for off in range(1, dp):
            send_piece(c, (me + off) % dp).wait_send()
        for off in range(1, tensor):
            send_term(c, (col + off) % tensor).wait_send()

    each(chunks, settle_chunk)


def fused(policy, ref_weight, tokens, gain, dp, tensor, chunks, model):
    _, piece_rows, _ = policy.shape
    local, columns = ref_weight.shape
    micros, per_micro, features = tokens.shape
    rows = micros * per_micro
    per_owner = dp // tensor
    width = columns // chunks
    bf16, f32 = jnp.bfloat16, jnp.float32
    plan = (dp, tensor, chunks, width, model)
    dma = pltpu.SemaphoreType.DMA
    blended, activated = pl.pallas_call(
        functools.partial(fused_kernel, plan),
        out_shape=[
            jax.ShapeDtypeStruct((dp, piece_rows, columns), bf16),
            jax.ShapeDtypeStruct((micros, per_owner * per_micro, columns), bf16),
        ],
        in_specs=[
            pl.BlockSpec(memory_space=pltpu.HBM),
            pl.BlockSpec(memory_space=pltpu.HBM),
            pl.BlockSpec(memory_space=pltpu.HBM),
            pl.BlockSpec(memory_space=pltpu.HBM),
        ],
        out_specs=[
            pl.BlockSpec(memory_space=pltpu.VMEM),
            pl.BlockSpec(memory_space=pltpu.VMEM),
        ],
        scratch_shapes=[
            pltpu.VMEM((chunks, dp, piece_rows, width), bf16),
            pltpu.VMEM((micros, per_micro, features), bf16),
            pltpu.VMEM((1, features), f32),
            pltpu.VMEM((tensor, rows, LANES), f32),
            pltpu.VMEM((dp, rows, features), bf16),
            pltpu.VMEM((chunks, dp, rows, width), bf16),
            pltpu.VMEM((chunks, tensor, per_owner, rows, width), bf16),
            dma((chunks, dp)),
            dma((chunks, dp)),
            dma((chunks,)),
            dma((chunks,)),
            dma,
            dma,
            dma((tensor,)),
            dma((tensor,)),
            dma((dp // 2,)),
            dma((dp // 2,)),
            dma((dp // 2,)),
            dma((dp,)),
            dma((chunks, tensor)),
            dma((chunks, tensor)),
        ],
        compiler_params=pltpu.CompilerParams(
            collective_id=0, has_side_effects=True, vmem_limit_bytes=40 * 1024 * 1024
        ),
        cost_estimate=pl.CostEstimate(
            flops=2 * dp * rows * features * columns,
            bytes_accessed=10 * local * columns,
            transcendentals=per_owner * rows * columns,
        ),
    )(
        policy.reshape(piece_rows, dp * columns),
        ref_weight.reshape(dp, piece_rows, columns),
        tokens,
        gain.reshape(1, features),
    )
    return blended.reshape(local, columns), activated


def plain(policy, ref_weight, tokens, gain, tensor, model):
    arrived = lax.all_to_all(policy, "dp", split_axis=2, concat_axis=0, tiled=True)
    new = arrived.reshape(ref_weight.shape).astype(jnp.float32)
    old = ref_weight.astype(jnp.float32)
    blended = (old + ema_rate * (new - old)).astype(jnp.bfloat16)
    pieces = []
    for micro in range(tokens.shape[0]):
        values = tokens[micro].astype(jnp.float32)
        total = lax.psum(jnp.sum(values * values, axis=1, keepdims=True), "tensor")
        normed = (values * lax.rsqrt(total / model + norm_eps) * gain).astype(jnp.bfloat16)
        normed = lax.all_gather(normed, "dp", axis=0, tiled=True)
        term = jnp.dot(normed, blended, preferred_element_type=jnp.float32)
        term = (term * (1.0 / math.sqrt(model))).astype(jnp.bfloat16)
        pieces.append(lax.psum_scatter(term, "tensor", scatter_dimension=0, tiled=True))
    gate = jnp.stack(pieces).astype(jnp.float32)
    return blended, jax.nn.silu(gate).astype(jnp.bfloat16)


def solution(mesh):
    dp, tensor = mesh.shape["dp"], mesh.shape["tensor"]

    def body(policy, ref_weight, tokens, gain):
        local, columns = ref_weight.shape
        model = local * tensor
        chunks = columns // 256
        fits = (
            dp % (2 * tensor) == 0
            and policy.shape[1] % 16 == 0
            and tokens.shape[1] % 16 == 0
            and columns % 256 == 0
            and chunks > dp // 2
            and dp // 2 >= AHEAD
        )
        if fits:
            return fused(policy, ref_weight, tokens, gain, dp, tensor, chunks, model)
        return plain(policy, ref_weight, tokens, gain, tensor, model)

    return jax.shard_map(
        body,
        mesh=mesh,
        in_specs=(P("dp", "tensor", None), P("tensor", "dp"), P(None, "dp", "tensor"), P("tensor")),
        out_specs=(P("tensor", "dp"), P(None, "tensor", "dp")),
        check_vma=False,
    )
```

```python
import functools
import math

import jax
import jax.numpy as jnp
from jax import lax
from jax.experimental import pallas as pl
from jax.experimental.pallas import tpu as pltpu
from jax.sharding import PartitionSpec as P

MESH = pl.DeviceIdType.MESH
LANES = 128
AHEAD = 2
HOP_STEPS = 2

ema_rate = 0.5
norm_eps = 1e-06


def each(count, step):
    lax.fori_loop(0, count, lambda i, _: (step(i), 0)[1], 0)


def fused_kernel(
    plan,
    policy,
    ref_in,
    tokens,
    gain,
    blended,
    activated,
    arrived,
    tok,
    gains,
    squares,
    gathered,
    partial,
    terms,
    piece_send,
    piece_recv,
    own_sem,
    ref_sem,
    tok_sem,
    gain_sem,
    square_send,
    square_recv,
    up_send,
    down_send,
    pair_send,
    block_recv,
    term_send,
    term_recv,
):
    dp, tensor, chunks, width, model = plan
    me = lax.axis_index("dp")
    col = lax.axis_index("tensor")
    levels = dp // 2
    level = me // 2
    core = me % 2
    pair = me + 1 - 2 * core
    per_owner = dp // tensor
    micros, per_micro, features = tokens.shape
    rows = micros * per_micro
    columns = chunks * width

    barrier = pltpu.get_barrier_semaphore()
    for off in range(1, dp):
        pl.semaphore_signal(
            barrier, inc=1, device_id={"dp": (me + off) % dp}, device_id_type=MESH
        )
    for off in range(1, tensor):
        pl.semaphore_signal(
            barrier, inc=1, device_id={"tensor": (col + off) % tensor}, device_id_type=MESH
        )

    def own_piece(c):
        return pltpu.make_async_copy(
            policy.at[:, pl.ds(pl.multiple_of(me * columns + c * width, width), width)],
            arrived.at[c, me],
            own_sem.at[c],
        )

    def part_of(c):
        return pl.ds(pl.multiple_of(c * width, width), width)

    def ref_piece(c):
        return pltpu.make_async_copy(
            ref_in.at[:, :, part_of(c)], blended.at[:, :, part_of(c)], ref_sem.at[c]
        )

    def send_piece(c, other):
        return pltpu.make_async_remote_copy(
            src_ref=policy.at[
                :, pl.ds(pl.multiple_of(other * columns + c * width, width), width)
            ],
            dst_ref=arrived.at[c, me],
            send_sem=piece_send.at[c, other],
            recv_sem=piece_recv.at[c, me],
            device_id={"dp": other},
            device_id_type=MESH,
        )

    def take_piece(c, other):
        return pltpu.make_async_remote_copy(
            src_ref=policy.at[:, pl.ds(0, width)],
            dst_ref=arrived.at[c, other],
            send_sem=piece_send.at[c, other],
            recv_sem=piece_recv.at[c, other],
            device_id={"dp": other},
            device_id_type=MESH,
        )

    def send_squares(other):
        return pltpu.make_async_remote_copy(
            src_ref=squares.at[col],
            dst_ref=squares.at[col],
            send_sem=square_send.at[other],
            recv_sem=square_recv.at[col],
            device_id={"tensor": other},
            device_id_type=MESH,
        )

    def take_squares(other):
        return pltpu.make_async_remote_copy(
            src_ref=squares.at[other],
            dst_ref=squares.at[other],
            send_sem=square_send.at[other],
            recv_sem=square_recv.at[other],
            device_id={"tensor": other},
            device_id_type=MESH,
        )

    def block_copy(block, sem, other):
        return pltpu.make_async_remote_copy(
            src_ref=gathered.at[block],
            dst_ref=gathered.at[block],
            send_sem=sem,
            recv_sem=block_recv.at[block],
            device_id={"dp": other},
            device_id_type=MESH,
        )

    def send_term(c, other):
        return pltpu.make_async_remote_copy(
            src_ref=partial.at[c, pl.ds(other * per_owner, per_owner)],
            dst_ref=terms.at[c, col],
            send_sem=term_send.at[c, other],
            recv_sem=term_recv.at[c, col],
            device_id={"tensor": other},
            device_id_type=MESH,
        )

    def take_term(c, other):
        return pltpu.make_async_remote_copy(
            src_ref=partial.at[c, pl.ds(other * per_owner, per_owner)],
            dst_ref=terms.at[c, other],
            send_sem=term_send.at[c, other],
            recv_sem=term_recv.at[c, other],
            device_id={"tensor": other},
            device_id_type=MESH,
        )

    tok_copy = pltpu.make_async_copy(tokens, tok, tok_sem)
    gain_copy = pltpu.make_async_copy(gain, gains, gain_sem)
    tok_copy.start()
    gain_copy.start()
    each(chunks, lambda c: ref_piece(c).start())
    each(chunks, lambda c: own_piece(c).start())
    tok_copy.wait()
    gain_copy.wait()
    for m in range(micros):
        total = jnp.zeros((per_micro, LANES), jnp.float32)
        for f in range(features // LANES):
            part = tok[m, :, f * LANES : (f + 1) * LANES].astype(jnp.float32)
            total = total + part * part
        squares[col, m * per_micro : (m + 1) * per_micro, :] = total
    pl.semaphore_wait(barrier, dp + tensor - 2)

    for off in range(1, tensor):
        send_squares((col + off) % tensor).start()

    order = sorted(range(1, dp), key=lambda off: abs(off - dp // 2))

    def send_chunk(c):
        for off in order:
            send_piece(c, (me + off) % dp).start()

    send_chunk(0)

    for off in range(1, tensor):
        take_squares((col + off) % tensor).wait_recv()
    for m in range(micros):
        total = squares[0, m * per_micro : (m + 1) * per_micro, :]
        for t in range(1, tensor):
            total = total + squares[t, m * per_micro : (m + 1) * per_micro, :]
        scale = lax.rsqrt(jnp.sum(total, axis=1, keepdims=True) / model + norm_eps)
        for f in range(0, features, 512):
            span = min(512, features - f)
            gathered[me, m * per_micro : (m + 1) * per_micro, f : f + span] = (
                tok[m, :, f : f + span].astype(jnp.float32) * scale * gains[:, f : f + span]
            ).astype(jnp.bfloat16)

    def relay(step, act):
        below = level - step
        above = level + step

        @pl.when(below >= 0)
        def _():
            block = 2 * below + core
            if step > 0:
                act("take", block_copy(block, up_send.at[step], me))

            @pl.when(level + 1 < levels)
            def _():
                act("send", block_copy(block, up_send.at[step], (me + 2) % dp))

            act("send", block_copy(block, pair_send.at[below], pair))

        @pl.when(above < levels)
        def _():
            block = 2 * above + core
            if step > 0:
                act("take", block_copy(block, down_send.at[step], me))
                act("send", block_copy(block, pair_send.at[above], pair))

            @pl.when(level > 0)
            def _():
                act("send", block_copy(block, down_send.at[step], (me + dp - 2) % dp))

    def forward(kind, copy):
        copy.wait_recv() if kind == "take" else copy.start()

    def settle(kind, copy):
        if kind == "send":
            copy.wait_send()

    relay(0, forward)
    for c in range(1, AHEAD):
        send_chunk(c)

    def take_chunk(c):
        ref_piece(c).wait()
        own_piece(c).wait()

        def blend(d):
            old = blended[d, :, part_of(c)].astype(jnp.float32)
            new = arrived[c, d].astype(jnp.float32)
            blended[d, :, part_of(c)] = (old + ema_rate * (new - old)).astype(jnp.bfloat16)

        blend(me)

        def take(i):
            other = (me + i + 1) % dp
            take_piece(c, other).wait_recv()
            blend(other)

        each(dp - 1, take)

    out_scale = 1.0 / math.sqrt(model)

    def multiply(c):
        left = gathered[...].reshape(dp * rows, features)
        right = blended[:, :, part_of(c)].reshape(features, width)
        product = jnp.dot(left, right, preferred_element_type=jnp.float32) * out_scale
        partial[c] = product.astype(jnp.bfloat16).reshape(dp, rows, width)
        for off in range(1, tensor):
            send_term(c, (col + off) % tensor).start()

    def finish(c):
        for off in range(1, tensor):
            take_term(c, (col + off) % tensor).wait_recv()
        for b in range(per_owner):
            gate = partial[c, col * per_owner + b].astype(jnp.float32)
            for off in range(1, tensor):
                gate = gate + terms[c, (col + off) % tensor, b].astype(jnp.float32)
            result = (gate / (1.0 + jnp.exp(-gate))).astype(jnp.bfloat16)
            for m in range(micros):
                activated[
                    m,
                    pl.ds(b * per_micro, per_micro),
                    part_of(c),
                ] = result[m * per_micro : (m + 1) * per_micro]

    early = HOP_STEPS * (levels - 1)
    late_steps = chunks - early
    per_step = -(-early // late_steps)
    for c in range(early):
        if c + AHEAD < chunks:
            send_chunk(c + AHEAD)
        take_chunk(c)
        if c % HOP_STEPS == 0:
            relay(c // HOP_STEPS + 1, forward)
    each(levels, lambda z: block_copy(2 * z + 1 - core, pair_send.at[z], pair).wait_recv())
    each(early, multiply)

    def late(c):
        c = c + early

        @pl.when(c + AHEAD < chunks)
        def _():
            send_chunk(c + AHEAD)

        take_chunk(c)
        multiply(c)
        first = per_step * (c - early)
        each(per_step, lambda i: pl.when(first + i < c)(lambda: finish(first + i)))

    each(late_steps, late)
    done = min(per_step * late_steps, chunks - 1)
    each(chunks - done, lambda i: finish(done + i))

    for off in range(1, tensor):
        send_squares((col + off) % tensor).wait_send()
    for step in range(levels):
        relay(step, settle)

    def settle_chunk(c):
        for off in range(1, dp):
            send_piece(c, (me + off) % dp).wait_send()
        for off in range(1, tensor):
            send_term(c, (col + off) % tensor).wait_send()

    each(chunks, settle_chunk)


def write_kernel(blended, activated, blended_out, activated_out, sems):
    count = sems.shape[0] - 1
    span = blended.shape[0] // count
    copies = [
        pltpu.make_async_copy(
            blended.at[pl.ds(i * span, span)], blended_out.at[pl.ds(i * span, span)], sems.at[i]
        )
        for i in range(count)
    ]
    copies.append(pltpu.make_async_copy(activated, activated_out, sems.at[count]))
    for copy in copies:
        copy.start()
    for copy in copies:
        copy.wait()


def write(blended, activated):
    return pl.pallas_call(
        write_kernel,
        out_shape=[
            jax.ShapeDtypeStruct(blended.shape, blended.dtype),
            jax.ShapeDtypeStruct(activated.shape, activated.dtype),
        ],
        in_specs=[pl.BlockSpec(memory_space=pltpu.VMEM)] * 2,
        out_specs=[pl.BlockSpec(memory_space=pltpu.HBM)] * 2,
        scratch_shapes=[pltpu.SemaphoreType.DMA((blended.shape[0] // 2 + 1,))],
        compiler_params=pltpu.CompilerParams(vmem_limit_bytes=16 * 1024 * 1024),
    )(blended, activated)


def fused(policy, ref_weight, tokens, gain, dp, tensor, chunks, model):
    _, piece_rows, _ = policy.shape
    local, columns = ref_weight.shape
    micros, per_micro, features = tokens.shape
    rows = micros * per_micro
    per_owner = dp // tensor
    width = columns // chunks
    bf16, f32 = jnp.bfloat16, jnp.float32
    plan = (dp, tensor, chunks, width, model)
    dma = pltpu.SemaphoreType.DMA
    blended, activated = pl.pallas_call(
        functools.partial(fused_kernel, plan),
        out_shape=[
            jax.ShapeDtypeStruct((dp, piece_rows, columns), bf16),
            jax.ShapeDtypeStruct((micros, per_owner * per_micro, columns), bf16),
        ],
        in_specs=[
            pl.BlockSpec(memory_space=pltpu.HBM),
            pl.BlockSpec(memory_space=pltpu.HBM),
            pl.BlockSpec(memory_space=pltpu.HBM),
            pl.BlockSpec(memory_space=pltpu.HBM),
        ],
        out_specs=[
            pl.BlockSpec(memory_space=pltpu.VMEM),
            pl.BlockSpec(memory_space=pltpu.VMEM),
        ],
        scratch_shapes=[
            pltpu.VMEM((chunks, dp, piece_rows, width), bf16),
            pltpu.VMEM((micros, per_micro, features), bf16),
            pltpu.VMEM((1, features), f32),
            pltpu.VMEM((tensor, rows, LANES), f32),
            pltpu.VMEM((dp, rows, features), bf16),
            pltpu.VMEM((chunks, dp, rows, width), bf16),
            pltpu.VMEM((chunks, tensor, per_owner, rows, width), bf16),
            dma((chunks, dp)),
            dma((chunks, dp)),
            dma((chunks,)),
            dma((chunks,)),
            dma,
            dma,
            dma((tensor,)),
            dma((tensor,)),
            dma((dp // 2,)),
            dma((dp // 2,)),
            dma((dp // 2,)),
            dma((dp,)),
            dma((chunks, tensor)),
            dma((chunks, tensor)),
        ],
        compiler_params=pltpu.CompilerParams(
            collective_id=0, has_side_effects=True, vmem_limit_bytes=40 * 1024 * 1024
        ),
        cost_estimate=pl.CostEstimate(
            flops=2 * dp * rows * features * columns,
            bytes_accessed=10 * local * columns,
            transcendentals=per_owner * rows * columns,
        ),
    )(
        policy.reshape(piece_rows, dp * columns),
        ref_weight.reshape(dp, piece_rows, columns),
        tokens,
        gain.reshape(1, features),
    )
    blended, activated = write(blended, activated)
    return blended.reshape(local, columns), activated


def plain(policy, ref_weight, tokens, gain, tensor, model):
    arrived = lax.all_to_all(policy, "dp", split_axis=2, concat_axis=0, tiled=True)
    new = arrived.reshape(ref_weight.shape).astype(jnp.float32)
    old = ref_weight.astype(jnp.float32)
    blended = (old + ema_rate * (new - old)).astype(jnp.bfloat16)
    pieces = []
    for micro in range(tokens.shape[0]):
        values = tokens[micro].astype(jnp.float32)
        total = lax.psum(jnp.sum(values * values, axis=1, keepdims=True), "tensor")
        normed = (values * lax.rsqrt(total / model + norm_eps) * gain).astype(jnp.bfloat16)
        normed = lax.all_gather(normed, "dp", axis=0, tiled=True)
        term = jnp.dot(normed, blended, preferred_element_type=jnp.float32)
        term = (term * (1.0 / math.sqrt(model))).astype(jnp.bfloat16)
        pieces.append(lax.psum_scatter(term, "tensor", scatter_dimension=0, tiled=True))
    gate = jnp.stack(pieces).astype(jnp.float32)
    return blended, jax.nn.silu(gate).astype(jnp.bfloat16)


def solution(mesh):
    dp, tensor = mesh.shape["dp"], mesh.shape["tensor"]

    def body(policy, ref_weight, tokens, gain):
        local, columns = ref_weight.shape
        model = local * tensor
        chunks = columns // 256
        fits = (
            dp % (2 * tensor) == 0
            and policy.shape[1] % 16 == 0
            and tokens.shape[1] % 16 == 0
            and columns % 256 == 0
            and HOP_STEPS * (dp // 2 - 1) in range(AHEAD, chunks)
        )
        if fits:
            return fused(policy, ref_weight, tokens, gain, dp, tensor, chunks, model)
        return plain(policy, ref_weight, tokens, gain, tensor, model)

    return jax.shard_map(
        body,
        mesh=mesh,
        in_specs=(P("dp", "tensor", None), P("tensor", "dp"), P(None, "dp", "tensor"), P("tensor")),
        out_specs=(P("tensor", "dp"), P(None, "tensor", "dp")),
        check_vma=False,
    )
```

```python
import functools
import math

import jax
import jax.numpy as jnp
from jax import lax
from jax.experimental import pallas as pl
from jax.experimental.pallas import tpu as pltpu
from jax.sharding import PartitionSpec as P

MESH = pl.DeviceIdType.MESH
LANES = 128
AHEAD = 2
HOP_STEPS = 1

ema_rate = 0.5
norm_eps = 1e-06


def each(count, step):
    lax.fori_loop(0, count, lambda i, _: (step(i), 0)[1], 0)


def fused_kernel(
    plan,
    policy,
    ref_in,
    tokens,
    gain,
    blended,
    activated,
    arrived,
    tok,
    gains,
    squares,
    gathered,
    partial,
    terms,
    piece_send,
    piece_recv,
    own_sem,
    ref_sem,
    tok_sem,
    gain_sem,
    square_send,
    square_recv,
    up_send,
    down_send,
    pair_send,
    block_recv,
    term_send,
    term_recv,
):
    dp, tensor, chunks, width, model = plan
    me = lax.axis_index("dp")
    col = lax.axis_index("tensor")
    levels = dp // 2
    level = me // 2
    core = me % 2
    pair = me + 1 - 2 * core
    per_owner = dp // tensor
    micros, per_micro, features = tokens.shape
    rows = micros * per_micro
    columns = chunks * width

    barrier = pltpu.get_barrier_semaphore()
    for off in range(1, dp):
        pl.semaphore_signal(
            barrier, inc=1, device_id={"dp": (me + off) % dp}, device_id_type=MESH
        )
    for off in range(1, tensor):
        pl.semaphore_signal(
            barrier, inc=1, device_id={"tensor": (col + off) % tensor}, device_id_type=MESH
        )

    def own_piece(c):
        return pltpu.make_async_copy(
            policy.at[:, pl.ds(pl.multiple_of(me * columns + c * width, width), width)],
            arrived.at[c, me],
            own_sem.at[c],
        )

    def part_of(c):
        return pl.ds(pl.multiple_of(c * width, width), width)

    def ref_piece(c):
        return pltpu.make_async_copy(
            ref_in.at[:, :, part_of(c)], blended.at[:, :, part_of(c)], ref_sem.at[c]
        )

    def send_piece(c, other):
        return pltpu.make_async_remote_copy(
            src_ref=policy.at[
                :, pl.ds(pl.multiple_of(other * columns + c * width, width), width)
            ],
            dst_ref=arrived.at[c, me],
            send_sem=piece_send.at[c, other],
            recv_sem=piece_recv.at[c, me],
            device_id={"dp": other},
            device_id_type=MESH,
        )

    def take_piece(c, other):
        return pltpu.make_async_remote_copy(
            src_ref=policy.at[:, pl.ds(0, width)],
            dst_ref=arrived.at[c, other],
            send_sem=piece_send.at[c, other],
            recv_sem=piece_recv.at[c, other],
            device_id={"dp": other},
            device_id_type=MESH,
        )

    def send_squares(other):
        return pltpu.make_async_remote_copy(
            src_ref=squares.at[col],
            dst_ref=squares.at[col],
            send_sem=square_send.at[other],
            recv_sem=square_recv.at[col],
            device_id={"tensor": other},
            device_id_type=MESH,
        )

    def take_squares(other):
        return pltpu.make_async_remote_copy(
            src_ref=squares.at[other],
            dst_ref=squares.at[other],
            send_sem=square_send.at[other],
            recv_sem=square_recv.at[other],
            device_id={"tensor": other},
            device_id_type=MESH,
        )

    def block_copy(block, sem, other):
        return pltpu.make_async_remote_copy(
            src_ref=gathered.at[block],
            dst_ref=gathered.at[block],
            send_sem=sem,
            recv_sem=block_recv.at[block],
            device_id={"dp": other},
            device_id_type=MESH,
        )

    def send_term(c, other):
        return pltpu.make_async_remote_copy(
            src_ref=partial.at[c, pl.ds(other * per_owner, per_owner)],
            dst_ref=terms.at[c, col],
            send_sem=term_send.at[c, other],
            recv_sem=term_recv.at[c, col],
            device_id={"tensor": other},
            device_id_type=MESH,
        )

    def take_term(c, other):
        return pltpu.make_async_remote_copy(
            src_ref=partial.at[c, pl.ds(other * per_owner, per_owner)],
            dst_ref=terms.at[c, other],
            send_sem=term_send.at[c, other],
            recv_sem=term_recv.at[c, other],
            device_id={"tensor": other},
            device_id_type=MESH,
        )

    tok_copy = pltpu.make_async_copy(tokens, tok, tok_sem)
    gain_copy = pltpu.make_async_copy(gain, gains, gain_sem)
    tok_copy.start()
    gain_copy.start()
    each(chunks, lambda c: ref_piece(c).start())
    each(chunks, lambda c: own_piece(c).start())
    tok_copy.wait()
    gain_copy.wait()
    for m in range(micros):
        total = jnp.zeros((per_micro, LANES), jnp.float32)
        for f in range(features // LANES):
            part = tok[m, :, f * LANES : (f + 1) * LANES].astype(jnp.float32)
            total = total + part * part
        squares[col, m * per_micro : (m + 1) * per_micro, :] = total
    pl.semaphore_wait(barrier, dp + tensor - 2)

    for off in range(1, tensor):
        send_squares((col + off) % tensor).start()

    half = dp // 2
    side = me // half

    def send_chunk(c):
        for i in range(half):
            send_piece(c, (1 - side) * half + (me + i) % half).start()
        for i in range(1, half):
            send_piece(c, side * half + (me + i) % half).start()

    send_chunk(0)

    for off in range(1, tensor):
        take_squares((col + off) % tensor).wait_recv()
    for m in range(micros):
        total = squares[0, m * per_micro : (m + 1) * per_micro, :]
        for t in range(1, tensor):
            total = total + squares[t, m * per_micro : (m + 1) * per_micro, :]
        scale = lax.rsqrt(jnp.sum(total, axis=1, keepdims=True) / model + norm_eps)
        for f in range(0, features, 512):
            span = min(512, features - f)
            gathered[me, m * per_micro : (m + 1) * per_micro, f : f + span] = (
                tok[m, :, f : f + span].astype(jnp.float32) * scale * gains[:, f : f + span]
            ).astype(jnp.bfloat16)

    def relay(step, act):
        below = level - step
        above = level + step

        @pl.when(below >= 0)
        def _():
            block = 2 * below + core
            if step > 0:
                act("take", block_copy(block, up_send.at[step], me))

            @pl.when(level + 1 < levels)
            def _():
                act("send", block_copy(block, up_send.at[step], (me + 2) % dp))

            act("send", block_copy(block, pair_send.at[below], pair))

        @pl.when(above < levels)
        def _():
            block = 2 * above + core
            if step > 0:
                act("take", block_copy(block, down_send.at[step], me))
                act("send", block_copy(block, pair_send.at[above], pair))

            @pl.when(level > 0)
            def _():
                act("send", block_copy(block, down_send.at[step], (me + dp - 2) % dp))

    def forward(kind, copy):
        copy.wait_recv() if kind == "take" else copy.start()

    def settle(kind, copy):
        if kind == "send":
            copy.wait_send()

    relay(0, forward)
    for c in range(1, AHEAD):
        send_chunk(c)

    def take_chunk(c):
        ref_piece(c).wait()
        own_piece(c).wait()

        def blend(d):
            old = blended[d, :, part_of(c)].astype(jnp.float32)
            new = arrived[c, d].astype(jnp.float32)
            blended[d, :, part_of(c)] = (old + ema_rate * (new - old)).astype(jnp.bfloat16)

        blend(me)

        def take(i):
            other = (me + i + 1) % dp
            take_piece(c, other).wait_recv()
            blend(other)

        each(dp - 1, take)

    out_scale = 1.0 / math.sqrt(model)

    def multiply(c):
        left = gathered[...].reshape(dp * rows, features)
        right = blended[:, :, part_of(c)].reshape(features, width)
        product = jnp.dot(left, right, preferred_element_type=jnp.float32) * out_scale
        partial[c] = product.astype(jnp.bfloat16).reshape(dp, rows, width)
        for off in range(1, tensor):
            send_term(c, (col + off) % tensor).start()

    def finish(c):
        for off in range(1, tensor):
            take_term(c, (col + off) % tensor).wait_recv()
        for b in range(per_owner):
            gate = partial[c, col * per_owner + b].astype(jnp.float32)
            for off in range(1, tensor):
                gate = gate + terms[c, (col + off) % tensor, b].astype(jnp.float32)
            result = (gate / (1.0 + jnp.exp(-gate))).astype(jnp.bfloat16)
            for m in range(micros):
                activated[
                    m,
                    pl.ds(b * per_micro, per_micro),
                    part_of(c),
                ] = result[m * per_micro : (m + 1) * per_micro]

    early = HOP_STEPS * (levels - 1) + 1
    late_steps = chunks - early
    per_step = -(-early // late_steps)
    for c in range(early):
        if c + AHEAD < chunks:
            send_chunk(c + AHEAD)
        take_chunk(c)
        if c % HOP_STEPS == 0 and c < early - 1:
            relay(c // HOP_STEPS + 1, forward)
    each(levels, lambda z: block_copy(2 * z + 1 - core, pair_send.at[z], pair).wait_recv())
    each(early, multiply)

    def late(c):
        c = c + early

        @pl.when(c + AHEAD < chunks)
        def _():
            send_chunk(c + AHEAD)

        take_chunk(c)
        multiply(c)
        first = per_step * (c - early)
        each(per_step, lambda i: pl.when(first + i < c)(lambda: finish(first + i)))

    each(late_steps, late)
    done = min(per_step * late_steps, chunks - 1)
    each(chunks - done, lambda i: finish(done + i))

    for off in range(1, tensor):
        send_squares((col + off) % tensor).wait_send()
    for step in range(levels):
        relay(step, settle)

    def settle_chunk(c):
        for off in range(1, dp):
            send_piece(c, (me + off) % dp).wait_send()
        for off in range(1, tensor):
            send_term(c, (col + off) % tensor).wait_send()

    each(chunks, settle_chunk)


def write_kernel(blended, activated, blended_out, activated_out, sems):
    count = sems.shape[0] - 1
    span = blended.shape[0] // count
    copies = [
        pltpu.make_async_copy(
            blended.at[pl.ds(i * span, span)], blended_out.at[pl.ds(i * span, span)], sems.at[i]
        )
        for i in range(count)
    ]
    copies.append(pltpu.make_async_copy(activated, activated_out, sems.at[count]))
    for copy in copies:
        copy.start()
    for copy in copies:
        copy.wait()


def write(blended, activated):
    return pl.pallas_call(
        write_kernel,
        out_shape=[
            jax.ShapeDtypeStruct(blended.shape, blended.dtype),
            jax.ShapeDtypeStruct(activated.shape, activated.dtype),
        ],
        in_specs=[pl.BlockSpec(memory_space=pltpu.VMEM)] * 2,
        out_specs=[pl.BlockSpec(memory_space=pltpu.HBM)] * 2,
        scratch_shapes=[pltpu.SemaphoreType.DMA((blended.shape[0] // 2 + 1,))],
        compiler_params=pltpu.CompilerParams(vmem_limit_bytes=16 * 1024 * 1024),
    )(blended, activated)


def fused(policy, ref_weight, tokens, gain, dp, tensor, chunks, model):
    _, piece_rows, _ = policy.shape
    local, columns = ref_weight.shape
    micros, per_micro, features = tokens.shape
    rows = micros * per_micro
    per_owner = dp // tensor
    width = columns // chunks
    bf16, f32 = jnp.bfloat16, jnp.float32
    plan = (dp, tensor, chunks, width, model)
    dma = pltpu.SemaphoreType.DMA
    blended, activated = pl.pallas_call(
        functools.partial(fused_kernel, plan),
        out_shape=[
            jax.ShapeDtypeStruct((dp, piece_rows, columns), bf16),
            jax.ShapeDtypeStruct((micros, per_owner * per_micro, columns), bf16),
        ],
        in_specs=[
            pl.BlockSpec(memory_space=pltpu.HBM),
            pl.BlockSpec(memory_space=pltpu.HBM),
            pl.BlockSpec(memory_space=pltpu.HBM),
            pl.BlockSpec(memory_space=pltpu.HBM),
        ],
        out_specs=[
            pl.BlockSpec(memory_space=pltpu.VMEM),
            pl.BlockSpec(memory_space=pltpu.VMEM),
        ],
        scratch_shapes=[
            pltpu.VMEM((chunks, dp, piece_rows, width), bf16),
            pltpu.VMEM((micros, per_micro, features), bf16),
            pltpu.VMEM((1, features), f32),
            pltpu.VMEM((tensor, rows, LANES), f32),
            pltpu.VMEM((dp, rows, features), bf16),
            pltpu.VMEM((chunks, dp, rows, width), bf16),
            pltpu.VMEM((chunks, tensor, per_owner, rows, width), bf16),
            dma((chunks, dp)),
            dma((chunks, dp)),
            dma((chunks,)),
            dma((chunks,)),
            dma,
            dma,
            dma((tensor,)),
            dma((tensor,)),
            dma((dp // 2,)),
            dma((dp // 2,)),
            dma((dp // 2,)),
            dma((dp,)),
            dma((chunks, tensor)),
            dma((chunks, tensor)),
        ],
        compiler_params=pltpu.CompilerParams(
            collective_id=0, has_side_effects=True, vmem_limit_bytes=40 * 1024 * 1024
        ),
        cost_estimate=pl.CostEstimate(
            flops=2 * dp * rows * features * columns,
            bytes_accessed=10 * local * columns,
            transcendentals=per_owner * rows * columns,
        ),
    )(
        policy.reshape(piece_rows, dp * columns),
        ref_weight.reshape(dp, piece_rows, columns),
        tokens,
        gain.reshape(1, features),
    )
    blended, activated = write(blended, activated)
    return blended.reshape(local, columns), activated


def plain(policy, ref_weight, tokens, gain, tensor, model):
    arrived = lax.all_to_all(policy, "dp", split_axis=2, concat_axis=0, tiled=True)
    new = arrived.reshape(ref_weight.shape).astype(jnp.float32)
    old = ref_weight.astype(jnp.float32)
    blended = (old + ema_rate * (new - old)).astype(jnp.bfloat16)
    pieces = []
    for micro in range(tokens.shape[0]):
        values = tokens[micro].astype(jnp.float32)
        total = lax.psum(jnp.sum(values * values, axis=1, keepdims=True), "tensor")
        normed = (values * lax.rsqrt(total / model + norm_eps) * gain).astype(jnp.bfloat16)
        normed = lax.all_gather(normed, "dp", axis=0, tiled=True)
        term = jnp.dot(normed, blended, preferred_element_type=jnp.float32)
        term = (term * (1.0 / math.sqrt(model))).astype(jnp.bfloat16)
        pieces.append(lax.psum_scatter(term, "tensor", scatter_dimension=0, tiled=True))
    gate = jnp.stack(pieces).astype(jnp.float32)
    return blended, jax.nn.silu(gate).astype(jnp.bfloat16)


def solution(mesh):
    dp, tensor = mesh.shape["dp"], mesh.shape["tensor"]

    def body(policy, ref_weight, tokens, gain):
        local, columns = ref_weight.shape
        model = local * tensor
        chunks = columns // 256
        fits = (
            dp % (2 * tensor) == 0
            and policy.shape[1] % 16 == 0
            and tokens.shape[1] % 16 == 0
            and columns % 256 == 0
            and HOP_STEPS * (dp // 2 - 1) + 1 in range(AHEAD, chunks)
        )
        if fits:
            return fused(policy, ref_weight, tokens, gain, dp, tensor, chunks, model)
        return plain(policy, ref_weight, tokens, gain, tensor, model)

    return jax.shard_map(
        body,
        mesh=mesh,
        in_specs=(P("dp", "tensor", None), P("tensor", "dp"), P(None, "dp", "tensor"), P("tensor")),
        out_specs=(P("tensor", "dp"), P(None, "tensor", "dp")),
        check_vma=False,
    )
```

```python
import functools
import math

import jax
import jax.numpy as jnp
from jax import lax
from jax.experimental import pallas as pl
from jax.experimental.pallas import tpu as pltpu
from jax.sharding import PartitionSpec as P

MESH = pl.DeviceIdType.MESH
LANES = 128
AHEAD = 3
HOP_STEPS = 1

ema_rate = 0.5
norm_eps = 1e-06


def each(count, step):
    lax.fori_loop(0, count, lambda i, _: (step(i), 0)[1], 0)


def fused_kernel(
    plan,
    policy,
    ref_in,
    tokens,
    gain,
    blended,
    activated,
    arrived,
    tok,
    gains,
    squares,
    gathered,
    partial,
    terms,
    piece_send,
    piece_recv,
    own_sem,
    ref_sem,
    tok_sem,
    gain_sem,
    square_send,
    square_recv,
    up_send,
    down_send,
    pair_send,
    block_recv,
    term_send,
    term_recv,
):
    dp, tensor, chunks, width, model = plan
    me = lax.axis_index("dp")
    col = lax.axis_index("tensor")
    levels = dp // 2
    level = me // 2
    core = me % 2
    pair = me + 1 - 2 * core
    per_owner = dp // tensor
    micros, per_micro, features = tokens.shape
    rows = micros * per_micro
    columns = chunks * width

    barrier = pltpu.get_barrier_semaphore()
    for off in range(1, dp):
        pl.semaphore_signal(
            barrier, inc=1, device_id={"dp": (me + off) % dp}, device_id_type=MESH
        )
    for off in range(1, tensor):
        pl.semaphore_signal(
            barrier, inc=1, device_id={"tensor": (col + off) % tensor}, device_id_type=MESH
        )

    def own_piece(c):
        return pltpu.make_async_copy(
            policy.at[:, pl.ds(pl.multiple_of(me * columns + c * width, width), width)],
            arrived.at[c, me],
            own_sem.at[c],
        )

    def part_of(c):
        return pl.ds(pl.multiple_of(c * width, width), width)

    def ref_piece(c):
        return pltpu.make_async_copy(
            ref_in.at[:, :, part_of(c)], blended.at[:, :, part_of(c)], ref_sem.at[c]
        )

    def send_piece(c, other):
        return pltpu.make_async_remote_copy(
            src_ref=policy.at[
                :, pl.ds(pl.multiple_of(other * columns + c * width, width), width)
            ],
            dst_ref=arrived.at[c, me],
            send_sem=piece_send.at[c, other],
            recv_sem=piece_recv.at[c, me],
            device_id={"dp": other},
            device_id_type=MESH,
        )

    def take_piece(c, other):
        return pltpu.make_async_remote_copy(
            src_ref=policy.at[:, pl.ds(0, width)],
            dst_ref=arrived.at[c, other],
            send_sem=piece_send.at[c, other],
            recv_sem=piece_recv.at[c, other],
            device_id={"dp": other},
            device_id_type=MESH,
        )

    def send_squares(other):
        return pltpu.make_async_remote_copy(
            src_ref=squares.at[col],
            dst_ref=squares.at[col],
            send_sem=square_send.at[other],
            recv_sem=square_recv.at[col],
            device_id={"tensor": other},
            device_id_type=MESH,
        )

    def take_squares(other):
        return pltpu.make_async_remote_copy(
            src_ref=squares.at[other],
            dst_ref=squares.at[other],
            send_sem=square_send.at[other],
            recv_sem=square_recv.at[other],
            device_id={"tensor": other},
            device_id_type=MESH,
        )

    def block_copy(block, sem, other):
        return pltpu.make_async_remote_copy(
            src_ref=gathered.at[block],
            dst_ref=gathered.at[block],
            send_sem=sem,
            recv_sem=block_recv.at[block],
            device_id={"dp": other},
            device_id_type=MESH,
        )

    def send_term(c, other):
        return pltpu.make_async_remote_copy(
            src_ref=partial.at[c, pl.ds(other * per_owner, per_owner)],
            dst_ref=terms.at[c, col],
            send_sem=term_send.at[c, other],
            recv_sem=term_recv.at[c, col],
            device_id={"tensor": other},
            device_id_type=MESH,
        )

    def take_term(c, other):
        return pltpu.make_async_remote_copy(
            src_ref=partial.at[c, pl.ds(other * per_owner, per_owner)],
            dst_ref=terms.at[c, other],
            send_sem=term_send.at[c, other],
            recv_sem=term_recv.at[c, other],
            device_id={"tensor": other},
            device_id_type=MESH,
        )

    tok_copy = pltpu.make_async_copy(tokens, tok, tok_sem)
    gain_copy = pltpu.make_async_copy(gain, gains, gain_sem)
    tok_copy.start()
    gain_copy.start()
    each(chunks, lambda c: ref_piece(c).start())
    each(chunks, lambda c: own_piece(c).start())
    tok_copy.wait()
    gain_copy.wait()
    for m in range(micros):
        total = jnp.zeros((per_micro, LANES), jnp.float32)
        for f in range(features // LANES):
            part = tok[m, :, f * LANES : (f + 1) * LANES].astype(jnp.float32)
            total = total + part * part
        squares[col, m * per_micro : (m + 1) * per_micro, :] = total
    pl.semaphore_wait(barrier, dp + tensor - 2)

    for off in range(1, tensor):
        send_squares((col + off) % tensor).start()

    half = dp // 2
    side = me // half

    def send_chunk(c):
        for i in range(half):
            send_piece(c, (1 - side) * half + (me + i) % half).start()
        for i in range(1, half):
            send_piece(c, side * half + (me + i) % half).start()

    send_chunk(0)

    for off in range(1, tensor):
        take_squares((col + off) % tensor).wait_recv()
    for m in range(micros):
        total = squares[0, m * per_micro : (m + 1) * per_micro, :]
        for t in range(1, tensor):
            total = total + squares[t, m * per_micro : (m + 1) * per_micro, :]
        scale = lax.rsqrt(jnp.sum(total, axis=1, keepdims=True) / model + norm_eps)
        for f in range(0, features, 512):
            span = min(512, features - f)
            gathered[me, m * per_micro : (m + 1) * per_micro, f : f + span] = (
                tok[m, :, f : f + span].astype(jnp.float32) * scale * gains[:, f : f + span]
            ).astype(jnp.bfloat16)

    def relay(step, act):
        below = level - step
        above = level + step

        @pl.when(below >= 0)
        def _():
            block = 2 * below + core
            if step > 0:
                act("take", block_copy(block, up_send.at[step], me))

            @pl.when(level + 1 < levels)
            def _():
                act("send", block_copy(block, up_send.at[step], (me + 2) % dp))

            act("send", block_copy(block, pair_send.at[below], pair))

        @pl.when(above < levels)
        def _():
            block = 2 * above + core
            if step > 0:
                act("take", block_copy(block, down_send.at[step], me))
                act("send", block_copy(block, pair_send.at[above], pair))

            @pl.when(level > 0)
            def _():
                act("send", block_copy(block, down_send.at[step], (me + dp - 2) % dp))

    def forward(kind, copy):
        copy.wait_recv() if kind == "take" else copy.start()

    def settle(kind, copy):
        if kind == "send":
            copy.wait_send()

    relay(0, forward)
    for c in range(1, AHEAD):
        send_chunk(c)

    def take_chunk(c):
        ref_piece(c).wait()
        own_piece(c).wait()

        def blend(d):
            old = blended[d, :, part_of(c)].astype(jnp.float32)
            new = arrived[c, d].astype(jnp.float32)
            blended[d, :, part_of(c)] = (old + ema_rate * (new - old)).astype(jnp.bfloat16)

        blend(me)

        def take(i):
            other = (me + i + 1) % dp
            take_piece(c, other).wait_recv()
            blend(other)

        each(dp - 1, take)

    out_scale = 1.0 / math.sqrt(model)

    def multiply(c):
        left = gathered[...].reshape(dp * rows, features)
        right = blended[:, :, part_of(c)].reshape(features, width)
        product = jnp.dot(left, right, preferred_element_type=jnp.float32) * out_scale
        partial[c] = product.astype(jnp.bfloat16).reshape(dp, rows, width)
        for off in range(1, tensor):
            send_term(c, (col + off) % tensor).start()

    def finish(c):
        for off in range(1, tensor):
            take_term(c, (col + off) % tensor).wait_recv()
        for b in range(per_owner):
            gate = partial[c, col * per_owner + b].astype(jnp.float32)
            for off in range(1, tensor):
                gate = gate + terms[c, (col + off) % tensor, b].astype(jnp.float32)
            result = (gate / (1.0 + jnp.exp(-gate))).astype(jnp.bfloat16)
            for m in range(micros):
                activated[
                    m,
                    pl.ds(b * per_micro, per_micro),
                    part_of(c),
                ] = result[m * per_micro : (m + 1) * per_micro]

    early = HOP_STEPS * (levels - 1) + 1
    late_steps = chunks - early
    per_step = -(-early // late_steps)
    for c in range(early):
        if c + AHEAD < chunks:
            send_chunk(c + AHEAD)
        take_chunk(c)
        if c % HOP_STEPS == 0 and c < early - 1:
            relay(c // HOP_STEPS + 1, forward)
    each(levels, lambda z: block_copy(2 * z + 1 - core, pair_send.at[z], pair).wait_recv())
    each(early, multiply)

    def late(c):
        c = c + early

        @pl.when(c + AHEAD < chunks)
        def _():
            send_chunk(c + AHEAD)

        take_chunk(c)
        multiply(c)
        first = per_step * (c - early)
        each(per_step, lambda i: pl.when(first + i < c)(lambda: finish(first + i)))

    each(late_steps, late)
    done = min(per_step * late_steps, chunks - 1)
    each(chunks - done, lambda i: finish(done + i))

    for off in range(1, tensor):
        send_squares((col + off) % tensor).wait_send()
    for step in range(levels):
        relay(step, settle)

    def settle_chunk(c):
        for off in range(1, dp):
            send_piece(c, (me + off) % dp).wait_send()
        for off in range(1, tensor):
            send_term(c, (col + off) % tensor).wait_send()

    each(chunks, settle_chunk)


def write_kernel(blended, activated, blended_out, activated_out, sems):
    count = sems.shape[0] - 1
    span = blended.shape[0] // count
    copies = [
        pltpu.make_async_copy(
            blended.at[pl.ds(i * span, span)], blended_out.at[pl.ds(i * span, span)], sems.at[i]
        )
        for i in range(count)
    ]
    copies.append(pltpu.make_async_copy(activated, activated_out, sems.at[count]))
    for copy in copies:
        copy.start()
    for copy in copies:
        copy.wait()


def write(blended, activated):
    return pl.pallas_call(
        write_kernel,
        out_shape=[
            jax.ShapeDtypeStruct(blended.shape, blended.dtype),
            jax.ShapeDtypeStruct(activated.shape, activated.dtype),
        ],
        in_specs=[pl.BlockSpec(memory_space=pltpu.VMEM)] * 2,
        out_specs=[pl.BlockSpec(memory_space=pltpu.HBM)] * 2,
        scratch_shapes=[pltpu.SemaphoreType.DMA((blended.shape[0] + 1,))],
        compiler_params=pltpu.CompilerParams(vmem_limit_bytes=16 * 1024 * 1024),
    )(blended, activated)


def fused(policy, ref_weight, tokens, gain, dp, tensor, chunks, model):
    _, piece_rows, _ = policy.shape
    local, columns = ref_weight.shape
    micros, per_micro, features = tokens.shape
    rows = micros * per_micro
    per_owner = dp // tensor
    width = columns // chunks
    bf16, f32 = jnp.bfloat16, jnp.float32
    plan = (dp, tensor, chunks, width, model)
    dma = pltpu.SemaphoreType.DMA
    blended, activated = pl.pallas_call(
        functools.partial(fused_kernel, plan),
        out_shape=[
            jax.ShapeDtypeStruct((dp, piece_rows, columns), bf16),
            jax.ShapeDtypeStruct((micros, per_owner * per_micro, columns), bf16),
        ],
        in_specs=[
            pl.BlockSpec(memory_space=pltpu.HBM),
            pl.BlockSpec(memory_space=pltpu.HBM),
            pl.BlockSpec(memory_space=pltpu.HBM),
            pl.BlockSpec(memory_space=pltpu.HBM),
        ],
        out_specs=[
            pl.BlockSpec(memory_space=pltpu.VMEM),
            pl.BlockSpec(memory_space=pltpu.VMEM),
        ],
        scratch_shapes=[
            pltpu.VMEM((chunks, dp, piece_rows, width), bf16),
            pltpu.VMEM((micros, per_micro, features), bf16),
            pltpu.VMEM((1, features), f32),
            pltpu.VMEM((tensor, rows, LANES), f32),
            pltpu.VMEM((dp, rows, features), bf16),
            pltpu.VMEM((chunks, dp, rows, width), bf16),
            pltpu.VMEM((chunks, tensor, per_owner, rows, width), bf16),
            dma((chunks, dp)),
            dma((chunks, dp)),
            dma((chunks,)),
            dma((chunks,)),
            dma,
            dma,
            dma((tensor,)),
            dma((tensor,)),
            dma((dp // 2,)),
            dma((dp // 2,)),
            dma((dp // 2,)),
            dma((dp,)),
            dma((chunks, tensor)),
            dma((chunks, tensor)),
        ],
        compiler_params=pltpu.CompilerParams(
            collective_id=0, has_side_effects=True, vmem_limit_bytes=40 * 1024 * 1024
        ),
        cost_estimate=pl.CostEstimate(
            flops=2 * dp * rows * features * columns,
            bytes_accessed=10 * local * columns,
            transcendentals=per_owner * rows * columns,
        ),
    )(
        policy.reshape(piece_rows, dp * columns),
        ref_weight.reshape(dp, piece_rows, columns),
        tokens,
        gain.reshape(1, features),
    )
    blended, activated = write(blended, activated)
    return blended.reshape(local, columns), activated


def plain(policy, ref_weight, tokens, gain, tensor, model):
    arrived = lax.all_to_all(policy, "dp", split_axis=2, concat_axis=0, tiled=True)
    new = arrived.reshape(ref_weight.shape).astype(jnp.float32)
    old = ref_weight.astype(jnp.float32)
    blended = (old + ema_rate * (new - old)).astype(jnp.bfloat16)
    pieces = []
    for micro in range(tokens.shape[0]):
        values = tokens[micro].astype(jnp.float32)
        total = lax.psum(jnp.sum(values * values, axis=1, keepdims=True), "tensor")
        normed = (values * lax.rsqrt(total / model + norm_eps) * gain).astype(jnp.bfloat16)
        normed = lax.all_gather(normed, "dp", axis=0, tiled=True)
        term = jnp.dot(normed, blended, preferred_element_type=jnp.float32)
        term = (term * (1.0 / math.sqrt(model))).astype(jnp.bfloat16)
        pieces.append(lax.psum_scatter(term, "tensor", scatter_dimension=0, tiled=True))
    gate = jnp.stack(pieces).astype(jnp.float32)
    return blended, jax.nn.silu(gate).astype(jnp.bfloat16)


def solution(mesh):
    dp, tensor = mesh.shape["dp"], mesh.shape["tensor"]

    def body(policy, ref_weight, tokens, gain):
        local, columns = ref_weight.shape
        model = local * tensor
        chunks = columns // 256
        fits = (
            dp % (2 * tensor) == 0
            and policy.shape[1] % 16 == 0
            and tokens.shape[1] % 16 == 0
            and columns % 256 == 0
            and HOP_STEPS * (dp // 2 - 1) + 1 in range(AHEAD, chunks)
        )
        if fits:
            return fused(policy, ref_weight, tokens, gain, dp, tensor, chunks, model)
        return plain(policy, ref_weight, tokens, gain, tensor, model)

    return jax.shard_map(
        body,
        mesh=mesh,
        in_specs=(P("dp", "tensor", None), P("tensor", "dp"), P(None, "dp", "tensor"), P("tensor")),
        out_specs=(P("tensor", "dp"), P(None, "tensor", "dp")),
        check_vma=False,
    )
```

```python
import functools
import math

import jax
import jax.numpy as jnp
from jax import lax
from jax.experimental import pallas as pl
from jax.experimental.pallas import tpu as pltpu
from jax.sharding import PartitionSpec as P

MESH = pl.DeviceIdType.MESH
LANES = 128
AHEAD = 3
HOP_STEPS = 1

ema_rate = 0.5
norm_eps = 1e-06


def each(count, step):
    lax.fori_loop(0, count, lambda i, _: (step(i), 0)[1], 0)


def fused_kernel(
    plan,
    policy,
    ref_in,
    tokens,
    gain,
    blended,
    activated,
    arrived,
    tok,
    gains,
    squares,
    gathered,
    partial,
    terms,
    piece_send,
    piece_recv,
    own_sem,
    ref_sem,
    tok_sem,
    gain_sem,
    square_send,
    square_recv,
    up_send,
    down_send,
    pair_send,
    block_recv,
    term_send,
    term_recv,
):
    dp, tensor, chunks, width, model = plan
    me = lax.axis_index("dp")
    col = lax.axis_index("tensor")
    levels = dp // 2
    level = me // 2
    core = me % 2
    pair = me + 1 - 2 * core
    per_owner = dp // tensor
    micros, per_micro, features = tokens.shape
    rows = micros * per_micro
    columns = chunks * width

    barrier = pltpu.get_barrier_semaphore()
    for off in range(1, dp):
        pl.semaphore_signal(
            barrier, inc=1, device_id={"dp": (me + off) % dp}, device_id_type=MESH
        )
    for off in range(1, tensor):
        pl.semaphore_signal(
            barrier, inc=1, device_id={"tensor": (col + off) % tensor}, device_id_type=MESH
        )

    parts = chunks + 1

    def lanes_of(c):
        if isinstance(c, int) and c >= chunks - 1:
            return chunks - 1, (c - chunks + 1) * (width // 2), width // 2
        return c, 0, width

    def columns_of(c):
        chunk, first, size = lanes_of(c)
        return pl.ds(pl.multiple_of(chunk * width + first, 128), size)

    def buffer_lanes(c):
        chunk, first, size = lanes_of(c)
        return chunk, pl.ds(first, size)

    def own_piece(c):
        return pltpu.make_async_copy(
            policy.at[:, pl.ds(pl.multiple_of(me * columns + c * width, width), width)],
            arrived.at[c, me],
            own_sem.at[c],
        )

    def part_of(c):
        return pl.ds(pl.multiple_of(c * width, width), width)

    def ref_piece(c):
        return pltpu.make_async_copy(
            ref_in.at[:, :, part_of(c)], blended.at[:, :, part_of(c)], ref_sem.at[c]
        )

    def send_piece(c, other):
        chunk, lanes = buffer_lanes(c)
        _, first, size = lanes_of(c)
        start = pl.multiple_of(other * columns + chunk * width + first, 128)
        return pltpu.make_async_remote_copy(
            src_ref=policy.at[:, pl.ds(start, size)],
            dst_ref=arrived.at[chunk, me, :, lanes],
            send_sem=piece_send.at[c, other],
            recv_sem=piece_recv.at[c, me],
            device_id={"dp": other},
            device_id_type=MESH,
        )

    def take_piece(c, other):
        chunk, lanes = buffer_lanes(c)
        return pltpu.make_async_remote_copy(
            src_ref=policy.at[:, pl.ds(0, lanes_of(c)[2])],
            dst_ref=arrived.at[chunk, other, :, lanes],
            send_sem=piece_send.at[c, other],
            recv_sem=piece_recv.at[c, other],
            device_id={"dp": other},
            device_id_type=MESH,
        )

    def send_squares(other):
        return pltpu.make_async_remote_copy(
            src_ref=squares.at[col],
            dst_ref=squares.at[col],
            send_sem=square_send.at[other],
            recv_sem=square_recv.at[col],
            device_id={"tensor": other},
            device_id_type=MESH,
        )

    def take_squares(other):
        return pltpu.make_async_remote_copy(
            src_ref=squares.at[other],
            dst_ref=squares.at[other],
            send_sem=square_send.at[other],
            recv_sem=square_recv.at[other],
            device_id={"tensor": other},
            device_id_type=MESH,
        )

    def block_copy(block, sem, other):
        return pltpu.make_async_remote_copy(
            src_ref=gathered.at[block],
            dst_ref=gathered.at[block],
            send_sem=sem,
            recv_sem=block_recv.at[block],
            device_id={"dp": other},
            device_id_type=MESH,
        )

    def send_term(c, other):
        chunk, lanes = buffer_lanes(c)
        return pltpu.make_async_remote_copy(
            src_ref=partial.at[chunk, pl.ds(other * per_owner, per_owner), :, lanes],
            dst_ref=terms.at[chunk, col, :, :, lanes],
            send_sem=term_send.at[c, other],
            recv_sem=term_recv.at[c, col],
            device_id={"tensor": other},
            device_id_type=MESH,
        )

    def take_term(c, other):
        chunk, lanes = buffer_lanes(c)
        return pltpu.make_async_remote_copy(
            src_ref=partial.at[chunk, pl.ds(other * per_owner, per_owner), :, lanes],
            dst_ref=terms.at[chunk, other, :, :, lanes],
            send_sem=term_send.at[c, other],
            recv_sem=term_recv.at[c, other],
            device_id={"tensor": other},
            device_id_type=MESH,
        )

    tok_copy = pltpu.make_async_copy(tokens, tok, tok_sem)
    gain_copy = pltpu.make_async_copy(gain, gains, gain_sem)
    tok_copy.start()
    gain_copy.start()
    each(chunks, lambda c: ref_piece(c).start())
    each(chunks, lambda c: own_piece(c).start())
    tok_copy.wait()
    gain_copy.wait()
    for m in range(micros):
        total = jnp.zeros((per_micro, LANES), jnp.float32)
        for f in range(features // LANES):
            part = tok[m, :, f * LANES : (f + 1) * LANES].astype(jnp.float32)
            total = total + part * part
        squares[col, m * per_micro : (m + 1) * per_micro, :] = total
    pl.semaphore_wait(barrier, dp + tensor - 2)

    for off in range(1, tensor):
        send_squares((col + off) % tensor).start()

    half = dp // 2
    side = me // half

    def send_chunk(c):
        for i in range(half):
            send_piece(c, (1 - side) * half + (me + i) % half).start()
        for i in range(1, half):
            send_piece(c, side * half + (me + i) % half).start()

    send_chunk(0)

    for off in range(1, tensor):
        take_squares((col + off) % tensor).wait_recv()
    for m in range(micros):
        total = squares[0, m * per_micro : (m + 1) * per_micro, :]
        for t in range(1, tensor):
            total = total + squares[t, m * per_micro : (m + 1) * per_micro, :]
        scale = lax.rsqrt(jnp.sum(total, axis=1, keepdims=True) / model + norm_eps)
        for f in range(0, features, 512):
            span = min(512, features - f)
            gathered[me, m * per_micro : (m + 1) * per_micro, f : f + span] = (
                tok[m, :, f : f + span].astype(jnp.float32) * scale * gains[:, f : f + span]
            ).astype(jnp.bfloat16)

    def relay(step, act):
        below = level - step
        above = level + step

        @pl.when(below >= 0)
        def _():
            block = 2 * below + core
            if step > 0:
                act("take", block_copy(block, up_send.at[step], me))

            @pl.when(level + 1 < levels)
            def _():
                act("send", block_copy(block, up_send.at[step], (me + 2) % dp))

            act("send", block_copy(block, pair_send.at[below], pair))

        @pl.when(above < levels)
        def _():
            block = 2 * above + core
            if step > 0:
                act("take", block_copy(block, down_send.at[step], me))
                act("send", block_copy(block, pair_send.at[above], pair))

            @pl.when(level > 0)
            def _():
                act("send", block_copy(block, down_send.at[step], (me + dp - 2) % dp))

    def forward(kind, copy):
        copy.wait_recv() if kind == "take" else copy.start()

    def settle(kind, copy):
        if kind == "send":
            copy.wait_send()

    relay(0, forward)
    for c in range(1, AHEAD):
        send_chunk(c)

    def take_chunk(c):
        chunk, lanes = buffer_lanes(c)
        if c < chunks:
            ref_piece(chunk).wait()
            own_piece(chunk).wait()

        def blend(d):
            old = blended[d, :, columns_of(c)].astype(jnp.float32)
            new = arrived[chunk, d, :, lanes].astype(jnp.float32)
            blended[d, :, columns_of(c)] = (old + ema_rate * (new - old)).astype(jnp.bfloat16)

        blend(me)

        def take(i):
            other = (me + i + 1) % dp
            take_piece(c, other).wait_recv()
            blend(other)

        each(dp - 1, take)

    out_scale = 1.0 / math.sqrt(model)

    def multiply(c):
        left = gathered[...].reshape(dp * rows, features)
        chunk, lanes = buffer_lanes(c)
        size = lanes_of(c)[2]
        right = blended[:, :, columns_of(c)].reshape(features, size)
        product = jnp.dot(left, right, preferred_element_type=jnp.float32) * out_scale
        partial[chunk, :, :, lanes] = product.astype(jnp.bfloat16).reshape(dp, rows, size)
        for off in range(1, tensor):
            send_term(c, (col + off) % tensor).start()

    def finish(c):
        chunk, lanes = buffer_lanes(c)
        for off in range(1, tensor):
            take_term(c, (col + off) % tensor).wait_recv()
        for b in range(per_owner):
            gate = partial[chunk, col * per_owner + b, :, lanes].astype(jnp.float32)
            for off in range(1, tensor):
                gate = gate + terms[chunk, (col + off) % tensor, b, :, lanes].astype(jnp.float32)
            result = (gate / (1.0 + jnp.exp(-gate))).astype(jnp.bfloat16)
            for m in range(micros):
                activated[
                    m,
                    pl.ds(b * per_micro, per_micro),
                    columns_of(c),
                ] = result[m * per_micro : (m + 1) * per_micro]

    early = HOP_STEPS * (levels - 1) + 1
    for c in range(early):
        if c + AHEAD < parts:
            send_chunk(c + AHEAD)
        take_chunk(c)
        if c % HOP_STEPS == 0 and c < early - 1:
            relay(c // HOP_STEPS + 1, forward)
    each(levels, lambda z: block_copy(2 * z + 1 - core, pair_send.at[z], pair).wait_recv())
    each(early, multiply)

    for c in range(early, parts):
        if c + AHEAD < parts:
            send_chunk(c + AHEAD)
        take_chunk(c)
        multiply(c)
        finish(c - early)
    for c in range(parts - early, parts):
        finish(c)

    for off in range(1, tensor):
        send_squares((col + off) % tensor).wait_send()
    for step in range(levels):
        relay(step, settle)

    def settle_chunk(c):
        for off in range(1, dp):
            send_piece(c, (me + off) % dp).wait_send()
        for off in range(1, tensor):
            send_term(c, (col + off) % tensor).wait_send()

    each(chunks - 1, settle_chunk)
    for c in range(chunks - 1, parts):
        settle_chunk(c)


def write_kernel(blended, activated, blended_out, activated_out, sems):
    count = sems.shape[0] - 1
    span = blended.shape[0] // count
    copies = [
        pltpu.make_async_copy(
            blended.at[pl.ds(i * span, span)], blended_out.at[pl.ds(i * span, span)], sems.at[i]
        )
        for i in range(count)
    ]
    copies.append(pltpu.make_async_copy(activated, activated_out, sems.at[count]))
    for copy in copies:
        copy.start()
    for copy in copies:
        copy.wait()


def write(blended, activated):
    return pl.pallas_call(
        write_kernel,
        out_shape=[
            jax.ShapeDtypeStruct(blended.shape, blended.dtype),
            jax.ShapeDtypeStruct(activated.shape, activated.dtype),
        ],
        in_specs=[pl.BlockSpec(memory_space=pltpu.VMEM)] * 2,
        out_specs=[pl.BlockSpec(memory_space=pltpu.HBM)] * 2,
        scratch_shapes=[pltpu.SemaphoreType.DMA((blended.shape[0] + 1,))],
        compiler_params=pltpu.CompilerParams(vmem_limit_bytes=16 * 1024 * 1024),
    )(blended, activated)


def fused(policy, ref_weight, tokens, gain, dp, tensor, chunks, model):
    _, piece_rows, _ = policy.shape
    local, columns = ref_weight.shape
    micros, per_micro, features = tokens.shape
    rows = micros * per_micro
    per_owner = dp // tensor
    width = columns // chunks
    bf16, f32 = jnp.bfloat16, jnp.float32
    plan = (dp, tensor, chunks, width, model)
    dma = pltpu.SemaphoreType.DMA
    blended, activated = pl.pallas_call(
        functools.partial(fused_kernel, plan),
        out_shape=[
            jax.ShapeDtypeStruct((dp, piece_rows, columns), bf16),
            jax.ShapeDtypeStruct((micros, per_owner * per_micro, columns), bf16),
        ],
        in_specs=[
            pl.BlockSpec(memory_space=pltpu.HBM),
            pl.BlockSpec(memory_space=pltpu.HBM),
            pl.BlockSpec(memory_space=pltpu.HBM),
            pl.BlockSpec(memory_space=pltpu.HBM),
        ],
        out_specs=[
            pl.BlockSpec(memory_space=pltpu.VMEM),
            pl.BlockSpec(memory_space=pltpu.VMEM),
        ],
        scratch_shapes=[
            pltpu.VMEM((chunks, dp, piece_rows, width), bf16),
            pltpu.VMEM((micros, per_micro, features), bf16),
            pltpu.VMEM((1, features), f32),
            pltpu.VMEM((tensor, rows, LANES), f32),
            pltpu.VMEM((dp, rows, features), bf16),
            pltpu.VMEM((chunks, dp, rows, width), bf16),
            pltpu.VMEM((chunks, tensor, per_owner, rows, width), bf16),
            dma((chunks + 1, dp)),
            dma((chunks + 1, dp)),
            dma((chunks,)),
            dma((chunks,)),
            dma,
            dma,
            dma((tensor,)),
            dma((tensor,)),
            dma((dp // 2,)),
            dma((dp // 2,)),
            dma((dp // 2,)),
            dma((dp,)),
            dma((chunks + 1, tensor)),
            dma((chunks + 1, tensor)),
        ],
        compiler_params=pltpu.CompilerParams(
            collective_id=0, has_side_effects=True, vmem_limit_bytes=40 * 1024 * 1024
        ),
        cost_estimate=pl.CostEstimate(
            flops=2 * dp * rows * features * columns,
            bytes_accessed=10 * local * columns,
            transcendentals=per_owner * rows * columns,
        ),
    )(
        policy.reshape(piece_rows, dp * columns),
        ref_weight.reshape(dp, piece_rows, columns),
        tokens,
        gain.reshape(1, features),
    )
    blended, activated = write(blended, activated)
    return blended.reshape(local, columns), activated


def plain(policy, ref_weight, tokens, gain, tensor, model):
    arrived = lax.all_to_all(policy, "dp", split_axis=2, concat_axis=0, tiled=True)
    new = arrived.reshape(ref_weight.shape).astype(jnp.float32)
    old = ref_weight.astype(jnp.float32)
    blended = (old + ema_rate * (new - old)).astype(jnp.bfloat16)
    pieces = []
    for micro in range(tokens.shape[0]):
        values = tokens[micro].astype(jnp.float32)
        total = lax.psum(jnp.sum(values * values, axis=1, keepdims=True), "tensor")
        normed = (values * lax.rsqrt(total / model + norm_eps) * gain).astype(jnp.bfloat16)
        normed = lax.all_gather(normed, "dp", axis=0, tiled=True)
        term = jnp.dot(normed, blended, preferred_element_type=jnp.float32)
        term = (term * (1.0 / math.sqrt(model))).astype(jnp.bfloat16)
        pieces.append(lax.psum_scatter(term, "tensor", scatter_dimension=0, tiled=True))
    gate = jnp.stack(pieces).astype(jnp.float32)
    return blended, jax.nn.silu(gate).astype(jnp.bfloat16)


def solution(mesh):
    dp, tensor = mesh.shape["dp"], mesh.shape["tensor"]

    def body(policy, ref_weight, tokens, gain):
        local, columns = ref_weight.shape
        model = local * tensor
        chunks = columns // 256
        fits = (
            dp % (2 * tensor) == 0
            and policy.shape[1] % 16 == 0
            and tokens.shape[1] % 16 == 0
            and columns % 256 == 0
            and HOP_STEPS * (dp // 2 - 1) + 1 in range(AHEAD, chunks)
        )
        if fits:
            return fused(policy, ref_weight, tokens, gain, dp, tensor, chunks, model)
        return plain(policy, ref_weight, tokens, gain, tensor, model)

    return jax.shard_map(
        body,
        mesh=mesh,
        in_specs=(P("dp", "tensor", None), P("tensor", "dp"), P(None, "dp", "tensor"), P("tensor")),
        out_specs=(P("tensor", "dp"), P(None, "tensor", "dp")),
        check_vma=False,
    )
```

```python
import functools
import math

import jax
import jax.numpy as jnp
from jax import lax
from jax.experimental import pallas as pl
from jax.experimental.pallas import tpu as pltpu
from jax.sharding import PartitionSpec as P

MESH = pl.DeviceIdType.MESH
LANES = 128
AHEAD = 3
HOP_STEPS = 1

ema_rate = 0.5
norm_eps = 1e-06


def each(count, step):
    lax.fori_loop(0, count, lambda i, _: (step(i), 0)[1], 0)


def fused_kernel(
    plan,
    policy,
    ref_in,
    tokens,
    gain,
    blended,
    activated,
    arrived,
    tok,
    gains,
    squares,
    gathered,
    partial,
    terms,
    piece_send,
    piece_recv,
    own_sem,
    ref_sem,
    tok_sem,
    gain_sem,
    square_send,
    square_recv,
    up_send,
    down_send,
    pair_send,
    block_recv,
    term_send,
    term_recv,
):
    dp, tensor, chunks, width, model = plan
    me = lax.axis_index("dp")
    col = lax.axis_index("tensor")
    levels = dp // 2
    level = me // 2
    core = me % 2
    pair = me + 1 - 2 * core
    per_owner = dp // tensor
    micros, per_micro, features = tokens.shape
    rows = micros * per_micro
    columns = chunks * width

    barrier = pltpu.get_barrier_semaphore()
    for off in range(1, dp):
        pl.semaphore_signal(
            barrier, inc=1, device_id={"dp": (me + off) % dp}, device_id_type=MESH
        )
    for off in range(1, tensor):
        pl.semaphore_signal(
            barrier, inc=1, device_id={"tensor": (col + off) % tensor}, device_id_type=MESH
        )

    def own_piece(c):
        return pltpu.make_async_copy(
            policy.at[:, pl.ds(pl.multiple_of(me * columns + c * width, width), width)],
            arrived.at[c, me],
            own_sem.at[c],
        )

    def part_of(c):
        return pl.ds(pl.multiple_of(c * width, width), width)

    def ref_piece(c):
        return pltpu.make_async_copy(
            ref_in.at[:, :, part_of(c)], blended.at[:, :, part_of(c)], ref_sem.at[c]
        )

    def send_piece(c, other):
        return pltpu.make_async_remote_copy(
            src_ref=policy.at[
                :, pl.ds(pl.multiple_of(other * columns + c * width, width), width)
            ],
            dst_ref=arrived.at[c, me],
            send_sem=piece_send.at[c, other],
            recv_sem=piece_recv.at[c, me],
            device_id={"dp": other},
            device_id_type=MESH,
        )

    def take_piece(c, other):
        return pltpu.make_async_remote_copy(
            src_ref=policy.at[:, pl.ds(0, width)],
            dst_ref=arrived.at[c, other],
            send_sem=piece_send.at[c, other],
            recv_sem=piece_recv.at[c, other],
            device_id={"dp": other},
            device_id_type=MESH,
        )

    def send_squares(other):
        return pltpu.make_async_remote_copy(
            src_ref=squares.at[col],
            dst_ref=squares.at[col],
            send_sem=square_send.at[other],
            recv_sem=square_recv.at[col],
            device_id={"tensor": other},
            device_id_type=MESH,
        )

    def take_squares(other):
        return pltpu.make_async_remote_copy(
            src_ref=squares.at[other],
            dst_ref=squares.at[other],
            send_sem=square_send.at[other],
            recv_sem=square_recv.at[other],
            device_id={"tensor": other},
            device_id_type=MESH,
        )

    def block_copy(block, sem, other):
        return pltpu.make_async_remote_copy(
            src_ref=gathered.at[block],
            dst_ref=gathered.at[block],
            send_sem=sem,
            recv_sem=block_recv.at[block],
            device_id={"dp": other},
            device_id_type=MESH,
        )

    def send_term(c, other):
        return pltpu.make_async_remote_copy(
            src_ref=partial.at[c, pl.ds(other * per_owner, per_owner)],
            dst_ref=terms.at[c, col],
            send_sem=term_send.at[c, other],
            recv_sem=term_recv.at[c, col],
            device_id={"tensor": other},
            device_id_type=MESH,
        )

    def take_term(c, other):
        return pltpu.make_async_remote_copy(
            src_ref=partial.at[c, pl.ds(other * per_owner, per_owner)],
            dst_ref=terms.at[c, other],
            send_sem=term_send.at[c, other],
            recv_sem=term_recv.at[c, other],
            device_id={"tensor": other},
            device_id_type=MESH,
        )

    tok_copy = pltpu.make_async_copy(tokens, tok, tok_sem)
    gain_copy = pltpu.make_async_copy(gain, gains, gain_sem)
    tok_copy.start()
    gain_copy.start()
    each(chunks, lambda c: ref_piece(c).start())
    each(chunks, lambda c: own_piece(c).start())
    tok_copy.wait()
    gain_copy.wait()
    for m in range(micros):
        total = jnp.zeros((per_micro, LANES), jnp.float32)
        for f in range(features // LANES):
            part = tok[m, :, f * LANES : (f + 1) * LANES].astype(jnp.float32)
            total = total + part * part
        squares[col, m * per_micro : (m + 1) * per_micro, :] = total
    pl.semaphore_wait(barrier, dp + tensor - 2)

    for off in range(1, tensor):
        send_squares((col + off) % tensor).start()

    half = dp // 2
    side = me // half

    def send_chunk(c):
        for i in range(half):
            send_piece(c, (1 - side) * half + (me + i + c) % half).start()
        for i in range(1, half):
            send_piece(c, side * half + (me + i) % half).start()

    send_chunk(0)

    for off in range(1, tensor):
        take_squares((col + off) % tensor).wait_recv()
    for m in range(micros):
        total = squares[0, m * per_micro : (m + 1) * per_micro, :]
        for t in range(1, tensor):
            total = total + squares[t, m * per_micro : (m + 1) * per_micro, :]
        scale = lax.rsqrt(jnp.sum(total, axis=1, keepdims=True) / model + norm_eps)
        for f in range(0, features, 512):
            span = min(512, features - f)
            gathered[me, m * per_micro : (m + 1) * per_micro, f : f + span] = (
                tok[m, :, f : f + span].astype(jnp.float32) * scale * gains[:, f : f + span]
            ).astype(jnp.bfloat16)

    def relay(step, act):
        below = level - step
        above = level + step

        @pl.when(below >= 0)
        def _():
            block = 2 * below + core
            if step > 0:
                act("take", block_copy(block, up_send.at[step], me))

            @pl.when(level + 1 < levels)
            def _():
                act("send", block_copy(block, up_send.at[step], (me + 2) % dp))

            act("send", block_copy(block, pair_send.at[below], pair))

        @pl.when(above < levels)
        def _():
            block = 2 * above + core
            if step > 0:
                act("take", block_copy(block, down_send.at[step], me))
                act("send", block_copy(block, pair_send.at[above], pair))

            @pl.when(level > 0)
            def _():
                act("send", block_copy(block, down_send.at[step], (me + dp - 2) % dp))

    def forward(kind, copy):
        copy.wait_recv() if kind == "take" else copy.start()

    def settle(kind, copy):
        if kind == "send":
            copy.wait_send()

    relay(0, forward)
    for c in range(1, AHEAD):
        send_chunk(c)

    def take_chunk(c):
        ref_piece(c).wait()
        own_piece(c).wait()

        def blend(d):
            old = blended[d, :, part_of(c)].astype(jnp.float32)
            new = arrived[c, d].astype(jnp.float32)
            blended[d, :, part_of(c)] = (old + ema_rate * (new - old)).astype(jnp.bfloat16)

        blend(me)

        def take(i):
            other = (me + i + 1) % dp
            take_piece(c, other).wait_recv()
            blend(other)

        each(dp - 1, take)

    out_scale = 1.0 / math.sqrt(model)

    def multiply(c):
        left = gathered[...].reshape(dp * rows, features)
        right = blended[:, :, part_of(c)].reshape(features, width)
        product = jnp.dot(left, right, preferred_element_type=jnp.float32) * out_scale
        partial[c] = product.astype(jnp.bfloat16).reshape(dp, rows, width)
        for off in range(1, tensor):
            send_term(c, (col + off) % tensor).start()

    def finish(c):
        for off in range(1, tensor):
            take_term(c, (col + off) % tensor).wait_recv()
        for b in range(per_owner):
            gate = partial[c, col * per_owner + b].astype(jnp.float32)
            for off in range(1, tensor):
                gate = gate + terms[c, (col + off) % tensor, b].astype(jnp.float32)
            result = (gate / (1.0 + jnp.exp(-gate))).astype(jnp.bfloat16)
            for m in range(micros):
                activated[
                    m,
                    pl.ds(b * per_micro, per_micro),
                    part_of(c),
                ] = result[m * per_micro : (m + 1) * per_micro]

    early = HOP_STEPS * (levels - 1) + 1
    late_steps = chunks - early
    per_step = -(-early // late_steps)
    for c in range(early):
        if c + AHEAD < chunks:
            send_chunk(c + AHEAD)
        take_chunk(c)
        if c % HOP_STEPS == 0 and c < early - 1:
            relay(c // HOP_STEPS + 1, forward)
    each(levels, lambda z: block_copy(2 * z + 1 - core, pair_send.at[z], pair).wait_recv())
    each(early, multiply)

    def late(c):
        c = c + early

        @pl.when(c + AHEAD < chunks)
        def _():
            send_chunk(c + AHEAD)

        take_chunk(c)
        multiply(c)
        first = per_step * (c - early)
        each(per_step, lambda i: pl.when(first + i < c)(lambda: finish(first + i)))

    each(late_steps, late)
    done = min(per_step * late_steps, chunks - 1)
    each(chunks - done, lambda i: finish(done + i))

    for off in range(1, tensor):
        send_squares((col + off) % tensor).wait_send()
    for step in range(levels):
        relay(step, settle)

    def settle_chunk(c):
        for off in range(1, dp):
            send_piece(c, (me + off) % dp).wait_send()
        for off in range(1, tensor):
            send_term(c, (col + off) % tensor).wait_send()

    each(chunks, settle_chunk)


def write_kernel(blended, activated, blended_out, activated_out, sems):
    count = sems.shape[0] - 1
    span = blended.shape[0] // count
    copies = [
        pltpu.make_async_copy(
            blended.at[pl.ds(i * span, span)], blended_out.at[pl.ds(i * span, span)], sems.at[i]
        )
        for i in range(count)
    ]
    copies.append(pltpu.make_async_copy(activated, activated_out, sems.at[count]))
    for copy in copies:
        copy.start()
    for copy in copies:
        copy.wait()


def write(blended, activated):
    return pl.pallas_call(
        write_kernel,
        out_shape=[
            jax.ShapeDtypeStruct(blended.shape, blended.dtype),
            jax.ShapeDtypeStruct(activated.shape, activated.dtype),
        ],
        in_specs=[pl.BlockSpec(memory_space=pltpu.VMEM)] * 2,
        out_specs=[pl.BlockSpec(memory_space=pltpu.HBM)] * 2,
        scratch_shapes=[pltpu.SemaphoreType.DMA((blended.shape[0] + 1,))],
        compiler_params=pltpu.CompilerParams(vmem_limit_bytes=16 * 1024 * 1024),
    )(blended, activated)


def fused(policy, ref_weight, tokens, gain, dp, tensor, chunks, model):
    _, piece_rows, _ = policy.shape
    local, columns = ref_weight.shape
    micros, per_micro, features = tokens.shape
    rows = micros * per_micro
    per_owner = dp // tensor
    width = columns // chunks
    bf16, f32 = jnp.bfloat16, jnp.float32
    plan = (dp, tensor, chunks, width, model)
    dma = pltpu.SemaphoreType.DMA
    blended, activated = pl.pallas_call(
        functools.partial(fused_kernel, plan),
        out_shape=[
            jax.ShapeDtypeStruct((dp, piece_rows, columns), bf16),
            jax.ShapeDtypeStruct((micros, per_owner * per_micro, columns), bf16),
        ],
        in_specs=[
            pl.BlockSpec(memory_space=pltpu.HBM),
            pl.BlockSpec(memory_space=pltpu.HBM),
            pl.BlockSpec(memory_space=pltpu.HBM),
            pl.BlockSpec(memory_space=pltpu.HBM),
        ],
        out_specs=[
            pl.BlockSpec(memory_space=pltpu.VMEM),
            pl.BlockSpec(memory_space=pltpu.VMEM),
        ],
        scratch_shapes=[
            pltpu.VMEM((chunks, dp, piece_rows, width), bf16),
            pltpu.VMEM((micros, per_micro, features), bf16),
            pltpu.VMEM((1, features), f32),
            pltpu.VMEM((tensor, rows, LANES), f32),
            pltpu.VMEM((dp, rows, features), bf16),
            pltpu.VMEM((chunks, dp, rows, width), bf16),
            pltpu.VMEM((chunks, tensor, per_owner, rows, width), bf16),
            dma((chunks, dp)),
            dma((chunks, dp)),
            dma((chunks,)),
            dma((chunks,)),
            dma,
            dma,
            dma((tensor,)),
            dma((tensor,)),
            dma((dp // 2,)),
            dma((dp // 2,)),
            dma((dp // 2,)),
            dma((dp,)),
            dma((chunks, tensor)),
            dma((chunks, tensor)),
        ],
        compiler_params=pltpu.CompilerParams(
            collective_id=0, has_side_effects=True, vmem_limit_bytes=40 * 1024 * 1024
        ),
        cost_estimate=pl.CostEstimate(
            flops=2 * dp * rows * features * columns,
            bytes_accessed=10 * local * columns,
            transcendentals=per_owner * rows * columns,
        ),
    )(
        policy.reshape(piece_rows, dp * columns),
        ref_weight.reshape(dp, piece_rows, columns),
        tokens,
        gain.reshape(1, features),
    )
    blended, activated = write(blended, activated)
    return blended.reshape(local, columns), activated


def plain(policy, ref_weight, tokens, gain, tensor, model):
    arrived = lax.all_to_all(policy, "dp", split_axis=2, concat_axis=0, tiled=True)
    new = arrived.reshape(ref_weight.shape).astype(jnp.float32)
    old = ref_weight.astype(jnp.float32)
    blended = (old + ema_rate * (new - old)).astype(jnp.bfloat16)
    pieces = []
    for micro in range(tokens.shape[0]):
        values = tokens[micro].astype(jnp.float32)
        total = lax.psum(jnp.sum(values * values, axis=1, keepdims=True), "tensor")
        normed = (values * lax.rsqrt(total / model + norm_eps) * gain).astype(jnp.bfloat16)
        normed = lax.all_gather(normed, "dp", axis=0, tiled=True)
        term = jnp.dot(normed, blended, preferred_element_type=jnp.float32)
        term = (term * (1.0 / math.sqrt(model))).astype(jnp.bfloat16)
        pieces.append(lax.psum_scatter(term, "tensor", scatter_dimension=0, tiled=True))
    gate = jnp.stack(pieces).astype(jnp.float32)
    return blended, jax.nn.silu(gate).astype(jnp.bfloat16)


def solution(mesh):
    dp, tensor = mesh.shape["dp"], mesh.shape["tensor"]

    def body(policy, ref_weight, tokens, gain):
        local, columns = ref_weight.shape
        model = local * tensor
        chunks = columns // 256
        fits = (
            dp % (2 * tensor) == 0
            and policy.shape[1] % 16 == 0
            and tokens.shape[1] % 16 == 0
            and columns % 256 == 0
            and HOP_STEPS * (dp // 2 - 1) + 1 in range(AHEAD, chunks)
        )
        if fits:
            return fused(policy, ref_weight, tokens, gain, dp, tensor, chunks, model)
        return plain(policy, ref_weight, tokens, gain, tensor, model)

    return jax.shard_map(
        body,
        mesh=mesh,
        in_specs=(P("dp", "tensor", None), P("tensor", "dp"), P(None, "dp", "tensor"), P("tensor")),
        out_specs=(P("tensor", "dp"), P(None, "tensor", "dp")),
        check_vma=False,
    )
```
